768 devices in a mesh: section: 192 (over z, x, y_lo), dp: 4 (over y_hi, core).
Axes of the slice: x: 4, y: 8 (y_hi: 2, y_lo: 4; y = y_hi * 4 + y_lo), z: 12, core: 2. Of those that a mesh axis runs over, the one named last changes fastest.
Arguments:
- activations: bfloat16 [192, 4, 1, 14, 14, 1024], P('section', 'dp'), may hold values from -6 to 6
- incoming: bfloat16 [192, 4, 1, 14, 14, 1024], P('section', 'dp'), may hold values from -6 to 6
- saved: bfloat16 [2, 192, 4, 1, 14, 14, 1024], P(None, 'section', 'dp'), may hold values from -6 to 6
- images: bfloat16 [2, 4, 1, 14, 14, 1024], P(None, 'dp'), may hold values from -6 to 6
- head_grads: bfloat16 [2, 4, 1, 14, 14, 1024], P(None, 'dp'), may hold values from -6 to 6
- pw_weight: bfloat16 [192, 1024, 1024], P('section'), may hold values from -0.1875 to 0.1875
- dw_kernel: float32 [192, 25, 1024], P('section'), may hold values from -1.25 to 1.25
Outputs:
- act_out: bfloat16 [192, 4, 1, 14, 14, 1024], P('section', 'dp')
- grad_out: bfloat16 [192, 4, 1, 14, 14, 1024], P('section', 'dp')
- w_grad: float32 [192, 1024, 1024], P('section', 'dp')
- k_grad: float32 [192, 25, 1024], P('section', None, 'dp')
The draws below stay inside these ranges and needn't reach their ends.
All inputs are finite; a program needn't handle non-finite values.
Results may differ from the reference program's by a relative error of at most 0.013.
Values may be sent and summed in bfloat16 or wider, within the bound.
No kernel may reach another device: no remote copies, remote signals or barrier semaphores. Data moves between devices by JAX's collectives and lax.ppermute only.
A program may use at most 64 MiB of HBM per device.

```python
import jax
import jax.numpy as jnp
from jax import lax

C = 1024
HW = 14
KW = 5
TAPS = 25
TICKS = 2
IMGS = 1
SECTIONS = 192
REPL = 4
N_DP = 4


def steps_of(key, shape, cuts, low, largest):
    def one(dim, shards_of):
        draws = jax.random.uniform(jax.random.fold_in(jax.random.fold_in(key, 6), dim), (shards_of,), jnp.float32, low / len(cuts), largest / len(cuts))
        return jnp.repeat(jnp.exp(draws), shape[dim] // shards_of).reshape((-1,) + (1,) * (len(shape) - dim - 1))

    level = one(*cuts[0])
    for cut in cuts[1:]:
        level = level * one(*cut)
    return level


def centred(stream_key, extent, scale, limit, pieces=(), kind=jnp.bfloat16):
    entries = jax.random.normal(stream_key, extent, jnp.float32) * scale
    if len(pieces) > 0:
        entries = steps_of(stream_key, extent, pieces, -0.22, 0.18) * entries
    return jnp.clip(entries, min=-limit, max=limit).astype(kind)


def setup_inputs(seed: int = 0) -> dict:
    arg_keys = jax.random.split(jax.random.key(seed), 8)
    return {
        "activations": centred(arg_keys[0], (SECTIONS, REPL, IMGS, HW, HW, C), 1.0, 6.0, ((0, 192), (1, 4))),
        "incoming": centred(arg_keys[1], (SECTIONS, REPL, IMGS, HW, HW, C), 1.0, 6.0, ((0, 192), (1, 4))),
        "saved": centred(arg_keys[2], (TICKS, SECTIONS, REPL, IMGS, HW, HW, C), 1.0, 6.0, ((1, 192), (2, 4))),
        "images": centred(arg_keys[3], (TICKS, REPL, IMGS, HW, HW, C), 1.0, 6.0, ((1, 4),)),
        "head_grads": centred(arg_keys[4], (TICKS, REPL, IMGS, HW, HW, C), 1.0, 6.0, ((1, 4),)),
        "pw_weight": centred(arg_keys[5], (SECTIONS, C, C), C ** -0.5, 0.1875, ((0, 192),)),
        "dw_kernel": centred(arg_keys[6], (SECTIONS, TAPS, C), TAPS ** -0.5, 1.25, ((0, 192),), jnp.float32),
    }


def depth_conv(field, kernel):
    channels = field.shape[-1]
    taps = kernel.reshape(KW, KW, 1, channels).astype(field.dtype)
    return lax.conv_general_dilated(field, taps, (1, 1), ((2, 2), (2, 2)), dimension_numbers=("NHWC", "HWIO", "NHWC"), feature_group_count=channels, precision=lax.Precision.HIGHEST)


def depthwise(field, kernel):
    return depth_conv(field, kernel)


def depthwise_back(grad, kernel):
    flipped = kernel.reshape(KW, KW, -1)[::-1, ::-1].reshape(KW * KW, -1)
    return depth_conv(grad, flipped)


def kernel_terms(rectified, grad):
    count, size, size_two, channels = grad.shape
    lhs_field = jnp.transpose(rectified, (1, 2, 3, 0)).reshape(1, size, size_two, channels * count)
    rhs_field = jnp.transpose(grad, (1, 2, 0, 3)).astype(rectified.dtype)
    result = lax.conv_general_dilated(lhs_field, rhs_field, (1, 1), ((2, 2), (2, 2)), dimension_numbers=("NHWC", "HWIO", "NHWC"), feature_group_count=channels, precision=lax.Precision.HIGHEST)
    return result.reshape(KW * KW, channels)


def cell_forward(inputs, kernel, weight):
    channels = inputs.shape[-1]
    widened = inputs.astype(jnp.float32)
    rectified = jnp.maximum(widened, 0.0)
    mixed = depthwise(rectified, kernel).astype(jnp.bfloat16)
    branch = jnp.dot(mixed.reshape(-1, channels), weight, preferred_element_type=jnp.float32)
    return (widened + branch.reshape(inputs.shape)).astype(jnp.bfloat16)


def cell_backward(inputs, upstream, kernel, weight):
    channels = inputs.shape[-1]
    widened = inputs.astype(jnp.float32)
    rectified = jnp.maximum(widened, 0.0)
    mixed = depthwise(rectified, kernel).astype(jnp.bfloat16).reshape(-1, channels)
    grad_rows = upstream.reshape(-1, channels)
    grad_mixed = lax.dot_general(grad_rows, weight, (((1,), (1,)), ((), ())), preferred_element_type=jnp.float32).reshape(inputs.shape)
    grad_rect = depthwise_back(grad_mixed, kernel)
    kernel_term = kernel_terms(rectified, grad_mixed)
    grad_in = (upstream.astype(jnp.float32) + jnp.where(widened > 0, grad_rect, 0.0)).astype(jnp.bfloat16)
    return grad_in, mixed, grad_rows, kernel_term


def reference(activations, incoming, saved, images, head_grads, pw_weight, dw_kernel):
    sections, replicas, imgs, side, side_two, channels = activations.shape
    flat_shape = (replicas * imgs, side, side_two, channels)
    current = activations
    upstream = incoming
    mixed_list = []
    grads_list = []
    kernel_total = jnp.zeros((sections, dw_kernel.shape[1], channels), jnp.float32)
    for tick in range(TICKS):
        def forward_one(operands):
            inputs, kernel, weight = operands
            return cell_forward(inputs.reshape(flat_shape), kernel, weight).reshape(inputs.shape)

        result = lax.map(forward_one, (current, dw_kernel, pw_weight))

        def backward_one(operands):
            inputs, grads, kernel, weight = operands
            grad_in, mixed, grad_rows, kernel_term = cell_backward(inputs.reshape(flat_shape), grads.reshape(flat_shape), kernel, weight)
            return (grad_in.reshape(inputs.shape), mixed.reshape(replicas, -1, channels), grad_rows.reshape(replicas, -1, channels), kernel_term)

        grad_in, mixed, grad_rows, kernel_term = lax.map(backward_one, (saved[tick], upstream, dw_kernel, pw_weight))
        mixed_list.append(mixed)
        grads_list.append(grad_rows)
        kernel_total = kernel_total + kernel_term
        current = jnp.concatenate([images[tick][None], result[:-1]], axis=0)
        upstream = jnp.concatenate([grad_in[1:], head_grads[tick][None]], axis=0)
    mixed_all = jnp.concatenate(mixed_list, axis=2)
    grads_all = jnp.concatenate(grads_list, axis=2)
    scale = 1.0 / (N_DP * TICKS)

    def weight_one(operands):
        mixed_section, grads_section = operands

        def replica_term(pair):
            term = lax.dot_general(pair[0], pair[1], (((0,), (0,)), ((), ())), preferred_element_type=jnp.float32)
            rounded = lax.optimization_barrier(term.astype(jnp.bfloat16))
            return rounded.astype(jnp.float32)

        return jnp.sum(lax.map(replica_term, (mixed_section, grads_section)), axis=0)

    w_grad = lax.map(weight_one, (mixed_all, grads_all)) * scale
    k_grad = kernel_total * scale
    return current, upstream, w_grad, k_grad
```

```python
import jax
import jax.numpy as jnp
from jax import lax
from jax.experimental import pallas as pl
from jax.experimental.pallas import tpu as pltpu
from jax.sharding import PartitionSpec as P

KW = 5
TAPS = KW * KW
TICKS = 2
HW = 14
PIX = HW * HW
C = 1024
LANES = 128
GROUPS = C // LANES
ROW = HW * GROUPS
HALF = C // 2
QUARTER = C // 4
PAD_ROWS = (HW + KW - 1) * ROW
DENSE_ROWS = PIX * GROUPS
TOP = (KW // 2) * ROW

f32 = jnp.float32
bf16 = jnp.bfloat16


def cols(group):
    return slice(group * LANES, (group + 1) * LANES)


def zero_pad(spread):
    zeros = jnp.zeros((TOP, LANES), f32)
    spread[0:TOP, :] = zeros
    spread[PAD_ROWS - TOP : PAD_ROWS, :] = zeros


def tile_at(spread, pixel):
    return spread[pl.ds(pl.multiple_of(pixel * GROUPS, GROUPS), GROUPS), :]


def conv(padded, taps, emit, flip):
    def row(p, carry):
        acc = [None] * HW
        for a in range(KW):
            tiles = [tile_at(padded, (p + a) * HW + q) for q in range(HW)]
            for b in range(KW):
                index = KW * a + b
                tap = taps[TAPS - 1 - index if flip else index]
                for q in range(HW):
                    src = q + b - KW // 2
                    if 0 <= src < HW:
                        term = tiles[src] * tap
                        acc[q] = term if acc[q] is None else acc[q] + term
        for q in range(HW):
            emit(p * HW + q, acc[q])
        return carry

    lax.fori_loop(0, HW, row, 0)


def tap_sums(rect_padded, grad_padded):
    def row(p, acc):
        acc = list(acc)
        grads = [tile_at(grad_padded, (p + KW // 2) * HW + q) for q in range(HW)]
        for a in range(KW):
            tiles = [tile_at(rect_padded, (p + a) * HW + q) for q in range(HW)]
            for b in range(KW):
                index = KW * a + b
                for q in range(HW):
                    src = q + b - KW // 2
                    if 0 <= src < HW:
                        acc[index] = acc[index] + tiles[src] * grads[q]
        return tuple(acc)

    return lax.fori_loop(0, HW, row, (jnp.zeros((GROUPS, LANES), f32),) * TAPS)


def store_tile(dense):
    def emit(pixel, value):
        dense[pl.ds(pl.multiple_of(pixel * GROUPS, GROUPS), GROUPS), :] = value

    return emit


def spread_rows(padded, group, value):
    padded[pl.ds(TOP + group, PIX, stride=GROUPS), :] = value


def rows_of(dense, group):
    return dense[pl.ds(group, PIX, stride=GROUPS), :]


def pack_rows(image, dst):
    for p in range(HW):
        dst[p * HW : (p + 1) * HW, :] = image[p].astype(f32)


def widen_pair(pair, wide):
    def step(p, carry):
        wide[pl.ds(pl.multiple_of(p * HW * 16, 16), HW * 16), :] = (
            pair[pl.ds(p * HW, HW)].astype(f32).reshape(HW * 16, LANES)
        )
        return carry

    lax.fori_loop(0, HW, step, 0)


def pair_tick_spread(wide, tick):
    return wide[pl.ds(tick, DENSE_ROWS, stride=TICKS), :]


def pair_tick_rows(wide, tick, group):
    return wide[pl.ds(tick + TICKS * group, PIX, stride=TICKS * GROUPS), :]


def replace_at_edge(edge, pair_hbm, tick, pair, wide, rows, sem):
    @pl.when(edge)
    def _():
        copy = pltpu.make_async_copy(pair_hbm, pair, sem)
        copy.start()
        copy.wait()
        widen_pair(pair, wide)
        for group in range(GROUPS):
            rows[:, cols(group)] = pair_tick_rows(wide, tick, group)


def mix(rows, padded, dense, mixed, taps):
    zero_pad(padded)
    for group in range(GROUPS):
        spread_rows(padded, group, jnp.maximum(rows[:, cols(group)], 0.0))
    conv(padded, taps, store_tile(dense), False)
    for group in range(GROUPS):
        mixed[:, cols(group)] = rows_of(dense, group).astype(bf16)


def finish_forward(tick, weight, images, out, rows, mixed, pair, wide, sem):
    rows[...] += jnp.dot(mixed[...], weight[...], preferred_element_type=f32)
    last = lax.axis_index("section") == lax.axis_size("section") - 1
    replace_at_edge(last, images, tick, pair, wide, rows, sem)
    out[...] = rows[...].astype(bf16)


def forward_first(
    x_hbm, w_hbm, taps_hbm, images, out, weight, taps, x, rows, padded, dense, mixed, pair, wide, sems
):
    copies = [
        pltpu.make_async_copy(src, dst, sems.at[i])
        for i, (src, dst) in enumerate([(x_hbm, x), (taps_hbm, taps), (w_hbm, weight)])
    ]
    for copy in copies:
        copy.start()
    copies[0].wait()
    pack_rows(x, rows)
    copies[1].wait()
    mix(rows, padded, dense, mixed, taps)
    copies[2].wait()
    finish_forward(0, weight, images, out, rows, mixed, pair, wide, sems.at[3])


def forward_second(x, weight, taps, images, token, out, rows, padded, dense, mixed, pair, wide, sem):
    rows[...] = x[...].astype(f32)
    mix(rows, padded, dense, mixed, taps)
    finish_forward(1, weight, images, out, rows, mixed, pair, wide, sem)


def spread_grad(g, weight, grad_mixed):
    product = lax.dot_general(
        g[...], weight[...], (((1,), (1,)), ((), ())), preferred_element_type=f32
    )
    zero_pad(grad_mixed)
    for group in range(GROUPS):
        spread_rows(grad_mixed, group, product[:, cols(group)])


def finish_backward(tick, taps, wide, heads, out, grad_mixed, rows, dense, mask, pair, spare, sem):
    mask[...] = pair_tick_spread(wide, tick)

    def emit(pixel, value):
        keep = tile_at(mask, pixel) > 0.0
        store_tile(dense)(pixel, jnp.where(keep, value, 0.0))

    conv(grad_mixed, taps, emit, True)
    for group in range(GROUPS):
        rows[:, cols(group)] += rows_of(dense, group)
    first = lax.axis_index("section") == 0
    replace_at_edge(first, heads, tick, pair, spare, rows, sem)
    out[...] = rows[...].astype(bf16)


def backward_first(
    g_hbm, saved, heads, weight, taps, token, out, grad_mixed, wide, g_rows, g, rows, dense, mask, pair, spare, sems
):
    copies = [
        pltpu.make_async_copy(src, dst, sems.at[i])
        for i, (src, dst) in enumerate([(g_hbm, g), (saved, pair)])
    ]
    for copy in copies:
        copy.start()
    copies[0].wait()
    pack_rows(g, rows)
    g_rows[...] = rows[...].astype(bf16)
    spread_grad(g_rows, weight, grad_mixed)
    copies[1].wait()
    widen_pair(pair, wide)
    finish_backward(0, taps, wide, heads, out, grad_mixed, rows, dense, mask, pair, spare, sems.at[2])


def backward_second(
    g, wide, heads, weight, taps, token, out, grad_mixed, rows, dense, mask, pair, spare, sem
):
    rows[...] = g[...].astype(f32)
    spread_grad(g, weight, grad_mixed)
    finish_backward(1, taps, wide, heads, out, grad_mixed, rows, dense, mask, pair, spare, sem)


def factors_kernel(wide, g_rows, taps, token, keep, send, rows, padded, dense):
    core = lax.rem(lax.axis_index("dp"), 2)
    high = lax.div(lax.axis_index("dp"), 2)
    send[:, C : 2 * C] = g_rows[...]
    zero_pad(padded)
    for tick in range(TICKS):
        padded[TOP : TOP + DENSE_ROWS, :] = jnp.maximum(pair_tick_spread(wide, tick), 0.0)
        conv(padded, taps, store_tile(dense), False)
        for group in range(GROUPS):
            rows[:, cols(group)] = rows_of(dense, group)
        for place in range(2):
            side = high if place == 0 else 1 - high
            at = tick * HALF + place * QUARTER
            own = pl.multiple_of((side * 2 + core) * QUARTER, QUARTER)
            other = pl.multiple_of((side * 2 + 1 - core) * QUARTER, QUARTER)
            keep[:, at : at + QUARTER] = rows[:, pl.ds(own, QUARTER)].astype(bf16)
            send[:, at : at + QUARTER] = rows[:, pl.ds(other, QUARTER)].astype(bf16)


def weight_kernel(keep, g_own0, g_own1, peer, g_peer1, token, own, other):
    def term(factor, grads):
        return lax.dot_general(factor, grads, (((0,), (0,)), ((), ())), preferred_element_type=f32)

    for place in range(2):
        first = slice(place * QUARTER, (place + 1) * QUARTER)
        second = slice(HALF + place * QUARTER, HALF + (place + 1) * QUARTER)
        total = term(keep[:, first], g_own0[...])
        total += term(peer[:, first], peer[:, C : 2 * C])
        total += term(keep[:, second], g_own1[...])
        total += term(peer[:, second], g_peer1[...])
        if place == 0:
            own[...] = total
        else:
            other[...] = total.astype(bf16)


def taps_kernel(wide, grad0, grad1, token, out, padded):
    zero_pad(padded)
    for tick in range(TICKS):
        padded[TOP : TOP + DENSE_ROWS, :] = jnp.maximum(pair_tick_spread(wide, tick), 0.0)
        sums = tap_sums(padded, (grad0, grad1)[tick])
        for index in range(TAPS):
            if tick == 0:
                out[index] = sums[index]
            else:
                out[index] += sums[index]


def final_kernel(own, arrived, out):
    out[...] = (own[...] + arrived[...].astype(f32)) * (1.0 / (2 * 2 * TICKS))


def unpack_kernel(message, out):
    rows = message[...].astype(f32)
    for p in range(HW):
        out[p] = rows[p * HW : (p + 1) * HW, :].astype(bf16)


VMEM = pl.BlockSpec(memory_space=pltpu.VMEM)
HBM = pl.BlockSpec(memory_space=pltpu.HBM)
ANY = pl.BlockSpec(memory_space=pl.ANY)


def call(kernel, ins, out_shape, scratch, args, cost=1):
    return pl.pallas_call(
        kernel,
        in_specs=ins,
        out_specs=jax.tree.map(lambda _: VMEM, out_shape),
        out_shape=out_shape,
        scratch_shapes=scratch,
        compiler_params=pltpu.CompilerParams(vmem_limit_bytes=20 * 1024 * 1024),
        cost_estimate=pl.CostEstimate(flops=0, bytes_accessed=cost << 10, transcendentals=0),
    )(*args)


PAIR = pltpu.VMEM((PIX, TICKS * GROUPS, LANES), bf16)
WIDE = pltpu.VMEM((PIX * TICKS * GROUPS, LANES), f32)
ROWS = pltpu.VMEM((PIX, C), f32)
PADDED = pltpu.VMEM((PAD_ROWS, LANES), f32)
DENSE = pltpu.VMEM((DENSE_ROWS, LANES), f32)
MIXED = pltpu.VMEM((PIX, C), bf16)
TILED = pltpu.VMEM((HW, HW, C), bf16)
IMAGE = jax.ShapeDtypeStruct((HW, HW, C), bf16)
MESSAGE = jax.ShapeDtypeStruct((PIX, C), bf16)
GRAD = jax.ShapeDtypeStruct((PAD_ROWS, LANES), f32)


def sems(count):
    return pltpu.SemaphoreType.DMA((count,)) if count > 1 else pltpu.SemaphoreType.DMA


def in_hbm(array):
    return pltpu.with_memory_space_constraint(array, pltpu.HBM)


def pair_view(array):
    moved = jnp.transpose(array, (1, 2, 0, 3)).reshape(HW, HW, TICKS, GROUPS, LANES)
    return jnp.transpose(moved, (0, 1, 3, 2, 4)).reshape(PIX, TICKS * GROUPS, LANES)


def ring(value, axis, by):
    peers = lax.axis_size(axis)
    return lax.ppermute(value, axis, [(i, (i + by) % peers) for i in range(peers)])


def other_core(value):
    return lax.ppermute(value, "dp", [(0, 1), (1, 0), (2, 3), (3, 2)])


def other_chip(value):
    return lax.ppermute(value, "dp", [(0, 2), (2, 0), (1, 3), (3, 1)])


def per_device(activations, incoming, saved, images, head_grads, pw_weight, dw_kernel):
    weight = pw_weight[0]
    taps = dw_kernel[0].reshape(TAPS, GROUPS, LANES)
    saved_pair = pair_view(saved[:, 0, 0, 0])
    image_pair = pair_view(images[:, 0, 0])
    head_pair = pair_view(head_grads[:, 0, 0])

    out0, w, t = call(
        forward_first,
        [HBM] * 4,
        (MESSAGE, jax.ShapeDtypeStruct((C, C), bf16), jax.ShapeDtypeStruct((TAPS, GROUPS, LANES), f32)),
        [TILED, ROWS, PADDED, DENSE, MIXED, PAIR, WIDE, sems(4)],
        tuple(map(in_hbm, (activations[0, 0, 0], weight, taps, image_pair))),
    )
    act1 = ring(out0, "section", 1)
    grad_in0, mixed_grad0, wide, g0 = call(
        backward_first,
        [HBM] * 3 + [VMEM, VMEM, ANY],
        (MESSAGE, GRAD, jax.ShapeDtypeStruct(WIDE.shape, f32), MESSAGE),
        [TILED, ROWS, DENSE, DENSE, PAIR, WIDE, sems(3)],
        tuple(map(in_hbm, (incoming[0, 0, 0], saved_pair, head_pair))) + (w, t, out0),
    )
    g1 = ring(grad_in0, "section", -1)
    keep, send = call(
        factors_kernel,
        [VMEM, VMEM, VMEM, ANY],
        (MESSAGE, jax.ShapeDtypeStruct((PIX, 2 * C), bf16)),
        [ROWS, PADDED, DENSE],
        (wide, g0, t, grad_in0),
    )
    peer = other_core(send)

    out1 = call(
        forward_second,
        [VMEM] * 3 + [HBM, ANY],
        MESSAGE,
        [ROWS, PADDED, DENSE, MIXED, PAIR, WIDE, sems(1)],
        (act1, w, t, in_hbm(image_pair), keep),
        8192,
    )
    act2 = ring(out1, "section", 1)
    g1, _ = lax.optimization_barrier((g1, out1))
    g1_peer = other_core(g1)
    grad_in1, mixed_grad1 = call(
        backward_second,
        [VMEM, VMEM, HBM, VMEM, VMEM, ANY],
        (MESSAGE, GRAD),
        [ROWS, DENSE, DENSE, PAIR, WIDE, sems(1)],
        (g1, wide, in_hbm(head_pair), w, t, out1),
    )
    g2 = ring(grad_in1, "section", -1)

    own, other = call(
        weight_kernel,
        [VMEM] * 5 + [ANY],
        (jax.ShapeDtypeStruct((QUARTER, C), f32), jax.ShapeDtypeStruct((QUARTER, C), bf16)),
        [],
        (keep, g0, g1, peer, g1_peer, grad_in1),
    )
    arrived = other_chip(other)

    terms = call(
        taps_kernel,
        [VMEM, VMEM, VMEM, ANY],
        jax.ShapeDtypeStruct((TAPS, GROUPS, LANES), f32),
        [PADDED],
        (wide, mixed_grad0, mixed_grad1, other),
    )
    core = lax.axis_index("dp") % 2
    high = lax.axis_index("dp") // 2
    by_core = terms.reshape(TAPS, 2, 2, QUARTER)
    mine = lax.dynamic_index_in_dim(by_core, core, 2, False)
    theirs = lax.dynamic_index_in_dim(by_core, 1 - core, 2, False)
    chip = mine + other_core(theirs.astype(bf16)).astype(f32)
    keep_k = lax.dynamic_index_in_dim(chip, high, 1, False)
    send_k = lax.dynamic_index_in_dim(chip, 1 - high, 1, False)
    scale = 1.0 / (lax.axis_size("dp") * TICKS)
    k_grad = (keep_k + other_chip(send_k.astype(bf16)).astype(f32)) * scale
    act_out = call(unpack_kernel, [VMEM], IMAGE, [], (act2,))
    grad_out = call(unpack_kernel, [VMEM], IMAGE, [], (g2,))
    w_grad = call(
        final_kernel, [VMEM, VMEM], jax.ShapeDtypeStruct((QUARTER, C), f32), [], (own, arrived)
    )
    return (act_out[None, None, None], grad_out[None, None, None], w_grad[None], k_grad[None])


def solution(mesh):
    in_specs = (
        P("section", "dp", None, None, None, None),
        P("section", "dp", None, None, None, None),
        P(None, "section", "dp", None, None, None, None),
        P(None, "dp", None, None, None, None),
        P(None, "dp", None, None, None, None),
        P("section", None, None),
        P("section", None, None),
    )
    out_specs = (
        P("section", "dp", None, None, None, None),
        P("section", "dp", None, None, None, None),
        P("section", "dp", None),
        P("section", None, "dp"),
    )
    return jax.shard_map(
        per_device, mesh=mesh, in_specs=in_specs, out_specs=out_specs, check_vma=False
    )
```

```python
import functools

import jax
import jax.numpy as jnp
from jax import lax
from jax.experimental import pallas as pl
from jax.experimental.pallas import tpu as pltpu
from jax.sharding import PartitionSpec as P

KW = 5
TAPS = KW * KW
TICKS = 2
HW = 14
PIX = HW * HW
C = 1024
LANES = 128
GROUPS = C // LANES
ROW = HW * GROUPS
HALF = C // 2
QUARTER = C // 4
PAD_ROWS = (HW + KW - 1) * ROW
DENSE_ROWS = PIX * GROUPS
TOP = (KW // 2) * ROW

f32 = jnp.float32
bf16 = jnp.bfloat16


def cols(group):
    return slice(group * LANES, (group + 1) * LANES)


def zero_pad(spread):
    zeros = jnp.zeros((TOP, LANES), f32)
    spread[0:TOP, :] = zeros
    spread[PAD_ROWS - TOP : PAD_ROWS, :] = zeros


def tile_at(spread, pixel):
    return spread[pl.ds(pl.multiple_of(pixel * GROUPS, GROUPS), GROUPS), :]


def conv(padded, taps, emit, flip):
    def row(p, carry):
        acc = [None] * HW
        for a in range(KW):
            tiles = [tile_at(padded, (p + a) * HW + q) for q in range(HW)]
            for b in range(KW):
                index = KW * a + b
                tap = taps[TAPS - 1 - index if flip else index]
                for q in range(HW):
                    src = q + b - KW // 2
                    if 0 <= src < HW:
                        term = tiles[src] * tap
                        acc[q] = term if acc[q] is None else acc[q] + term
        for q in range(HW):
            emit(p * HW + q, acc[q])
        return carry

    lax.fori_loop(0, HW, row, 0)


def tap_sums(rect_padded, grad_padded):
    def row(p, acc):
        acc = list(acc)
        grads = [tile_at(grad_padded, (p + KW // 2) * HW + q) for q in range(HW)]
        for a in range(KW):
            tiles = [tile_at(rect_padded, (p + a) * HW + q) for q in range(HW)]
            for b in range(KW):
                index = KW * a + b
                for q in range(HW):
                    src = q + b - KW // 2
                    if 0 <= src < HW:
                        acc[index] = acc[index] + tiles[src] * grads[q]
        return tuple(acc)

    return lax.fori_loop(0, HW, row, (jnp.zeros((GROUPS, LANES), f32),) * TAPS)


def store_tile(dense):
    def emit(pixel, value):
        dense[pl.ds(pl.multiple_of(pixel * GROUPS, GROUPS), GROUPS), :] = value

    return emit


def spread_rows(padded, group, value):
    padded[pl.ds(TOP + group, PIX, stride=GROUPS), :] = value


def rows_of(dense, group):
    return dense[pl.ds(group, PIX, stride=GROUPS), :]


def pack_rows(image, dst):
    for p in range(HW):
        dst[p * HW : (p + 1) * HW, :] = image[p].astype(f32)


def widen_pair(pair, wide):
    def step(p, carry):
        wide[pl.ds(pl.multiple_of(p * HW * 16, 16), HW * 16), :] = (
            pair[pl.ds(p * HW, HW)].astype(f32).reshape(HW * 16, LANES)
        )
        return carry

    lax.fori_loop(0, HW, step, 0)


def pair_tick_spread(wide, tick):
    return wide[pl.ds(tick, DENSE_ROWS, stride=TICKS), :]


def pair_tick_rows(wide, tick, group):
    return wide[pl.ds(tick + TICKS * group, PIX, stride=TICKS * GROUPS), :]


def replace_at_edge(edge, pair_hbm, tick, pair, wide, rows, sem):
    @pl.when(edge)
    def _():
        fetch(pair_hbm, pair, sem)
        widen_pair(pair, wide)
        for group in range(GROUPS):
            rows[:, cols(group)] = pair_tick_rows(wide, tick, group).astype(rows.dtype)


def fetch(src, dst, sem):
    copy = pltpu.make_async_copy(src, dst, sem)
    copy.start()
    copy.wait()


def is_first():
    return lax.axis_index("section") == 0


def is_last():
    return lax.axis_index("section") == lax.axis_size("section") - 1


def mix(rows, padded, dense, mixed, taps):
    zero_pad(padded)
    for group in range(GROUPS):
        spread_rows(padded, group, jnp.maximum(rows[:, cols(group)], 0.0))
    conv(padded, taps, store_tile(dense), False)
    for group in range(GROUPS):
        mixed[:, cols(group)] = rows_of(dense, group).astype(bf16)


def forward_first(x_hbm, w_hbm, taps_hbm, out, weight, taps, x, rows, padded, dense, mixed, sems):
    copies = [
        pltpu.make_async_copy(src, dst, sems.at[i])
        for i, (src, dst) in enumerate([(x_hbm, x), (taps_hbm, taps), (w_hbm, weight)])
    ]
    for copy in copies:
        copy.start()
    copies[0].wait()
    pack_rows(x, rows)
    copies[1].wait()
    mix(rows, padded, dense, mixed, taps)
    copies[2].wait()
    out[...] = (rows[...] + jnp.dot(mixed[...], weight[...], preferred_element_type=f32)).astype(bf16)


def forward_second(x, weight, taps, images, token, out, rows, padded, dense, mixed, pair, wide, sem):
    rows[...] = x[...].astype(f32)
    replace_at_edge(is_first(), images, 0, pair, wide, rows, sem)
    mix(rows, padded, dense, mixed, taps)
    out[...] = (rows[...] + jnp.dot(mixed[...], weight[...], preferred_element_type=f32)).astype(bf16)


def head_kernel(g_in, heads, g_out, pair, wide, rows, sem):
    @pl.when(is_last())
    def _():
        fetch(heads, pair, sem)
        widen_pair(pair, wide)
        for group in range(GROUPS):
            rows[:, cols(group)] = pair_tick_rows(wide, 0, group).astype(bf16)
        fetch(rows, g_out, sem)


def spread_grad(g, weight, grad_mixed):
    product = lax.dot_general(
        g[...], weight[...], (((1,), (1,)), ((), ())), preferred_element_type=f32
    )
    zero_pad(grad_mixed)
    for group in range(GROUPS):
        spread_rows(grad_mixed, group, product[:, cols(group)])


def finish_backward(tick, taps, wide, out, grad_mixed, rows, dense, mask):
    mask[...] = pair_tick_spread(wide, tick)

    def emit(pixel, value):
        keep = tile_at(mask, pixel) > 0.0
        store_tile(dense)(pixel, jnp.where(keep, value, 0.0))

    conv(grad_mixed, taps, emit, True)
    for group in range(GROUPS):
        out[:, cols(group)] = (rows[:, cols(group)] + rows_of(dense, group)).astype(bf16)


def backward_first(
    g_hbm, saved, weight, taps, token, out, g_rows, g, rows, grad_mixed, dense, mask, pair, wide, sems
):
    copies = [
        pltpu.make_async_copy(src, dst, sems.at[i])
        for i, (src, dst) in enumerate([(g_hbm, g), (saved, pair)])
    ]
    for copy in copies:
        copy.start()
    copies[0].wait()
    pack_rows(g, rows)
    g_rows[...] = rows[...].astype(bf16)
    spread_grad(g_rows, weight, grad_mixed)
    copies[1].wait()
    widen_pair(pair, wide)
    finish_backward(0, taps, wide, out, grad_mixed, rows, dense, mask)


def backward_second(
    g, saved, weight, taps, token, out, rows, grad_mixed, dense, mask, pair, wide, sem
):
    copy = pltpu.make_async_copy(saved, pair, sem)
    copy.start()
    rows[...] = g[...].astype(f32)
    spread_grad(g, weight, grad_mixed)
    copy.wait()
    widen_pair(pair, wide)
    finish_backward(1, taps, wide, out, grad_mixed, rows, dense, mask)


def halves(core):
    return [2 * core, 2 * core + 1, 4 + 2 * core, 5 + 2 * core]


def factors_kernel(saved, taps, token, keep, send, keep_rect, rows, padded, dense, pair, wide, sem):
    core = lax.rem(lax.axis_index("dp"), 2)
    high = lax.div(lax.axis_index("dp"), 2)
    fetch(saved, pair, sem)
    widen_pair(pair, wide)
    zero_pad(padded)
    for tick in range(TICKS):
        padded[TOP : TOP + DENSE_ROWS, :] = jnp.maximum(pair_tick_spread(wide, tick), 0.0)
        for at, (mine, theirs) in enumerate(zip(halves(core), halves(1 - core))):
            place = tick * HALF + at * LANES
            keep_rect[:, place : place + LANES] = rows_of(padded, TOP + mine).astype(bf16)
            send[:, C + place : C + place + LANES] = rows_of(padded, TOP + theirs).astype(bf16)
        conv(padded, taps, store_tile(dense), False)
        for group in range(GROUPS):
            rows[:, cols(group)] = rows_of(dense, group)
        for place in range(2):
            side = high if place == 0 else 1 - high
            at = tick * HALF + place * QUARTER
            own = pl.multiple_of((side * 2 + core) * QUARTER, QUARTER)
            other = pl.multiple_of((side * 2 + 1 - core) * QUARTER, QUARTER)
            keep[:, at : at + QUARTER] = rows[:, pl.ds(own, QUARTER)].astype(bf16)
            send[:, at : at + QUARTER] = rows[:, pl.ds(other, QUARTER)].astype(bf16)


def weight_term(factor, grads):
    return lax.dot_general(factor, grads, (((0,), (0,)), ((), ())), preferred_element_type=f32)


def weight_first(keep, g_own, peer, g_peer, out):
    out[...] = weight_term(keep[:, :HALF], g_own[...])
    out[...] += weight_term(peer[:, :HALF], g_peer[...])


def weight_second(total, keep, g_own, peer, g_peer, own, other):
    for place in range(2):
        rows = slice(place * QUARTER, (place + 1) * QUARTER)
        part = slice(HALF + place * QUARTER, HALF + (place + 1) * QUARTER)
        value = total[rows, :] + weight_term(keep[:, part], g_own[...])
        value += weight_term(peer[:, part], g_peer[...])
        if place == 0:
            own[...] = value
        else:
            other[...] = value.astype(bf16)


def taps_kernel(keep_rect, peer, g0, g0_peer, g1, g1_peer, weight, token, own, far, rect, grad, sums):
    core = lax.rem(lax.axis_index("dp"), 2)
    high = lax.div(lax.axis_index("dp"), 2)
    zero_pad(rect)
    zero_pad(grad)
    sums[...] = jnp.zeros_like(sums)
    for tick in range(TICKS):
        grads = (g0, g1)[tick][...], (g0_peer, g1_peer)[tick][...]
        for image in range(2):
            for side in range(2):
                rows = weight[pl.ds(pl.multiple_of((2 * side + core) * QUARTER, QUARTER), QUARTER), :]
                product = lax.dot_general(
                    grads[image], rows, (((1,), (1,)), ((), ())), preferred_element_type=f32
                )
                for part in range(2):
                    at = 2 * side + part
                    spread_rows(grad, 4 * image + at, product[:, cols(part)])
                    place = tick * HALF + at * LANES
                    source = keep_rect if image == 0 else peer
                    place += 0 if image == 0 else C
                    spread_rows(rect, 4 * image + at, source[:, place : place + LANES].astype(f32))
        terms = tap_sums(rect, grad)
        for index in range(TAPS):
            both = terms[index][0:4] + terms[index][4:8]
            sums[index : index + 1, :HALF] += jnp.concatenate(
                [both[i : i + 1] for i in range(4)], axis=1
            )
    low, top = sums[0:TAPS, 0:QUARTER], sums[0:TAPS, QUARTER:HALF]
    own[...] = jnp.where(high == 0, low, top)
    far[...] = jnp.where(high == 0, top, low).astype(bf16)


def final_kernel(own, arrived, out):
    out[...] = (own[...] + arrived[...].astype(f32)) * (1.0 / (2 * 2 * TICKS))


def unpack_kernel(edge, message, images, out, rows, pair, wide, sem):
    rows[...] = message[...].astype(f32)
    replace_at_edge(edge(), images, 1, pair, wide, rows, sem)
    for p in range(HW):
        out[p] = rows[p * HW : (p + 1) * HW, :].astype(bf16)


VMEM = pl.BlockSpec(memory_space=pltpu.VMEM)
HBM = pl.BlockSpec(memory_space=pltpu.HBM)
ANY = pl.BlockSpec(memory_space=pl.ANY)


def call(kernel, ins, out_shape, scratch, args, cost=1, outs=None, **options):
    pinned = [in_hbm(arg) if spec is HBM else arg for spec, arg in zip(ins, args)]
    return pl.pallas_call(
        kernel,
        in_specs=ins,
        out_specs=jax.tree.map(lambda _: VMEM, out_shape) if outs is None else outs,
        out_shape=out_shape,
        scratch_shapes=scratch,
        compiler_params=pltpu.CompilerParams(vmem_limit_bytes=20 * 1024 * 1024),
        cost_estimate=pl.CostEstimate(flops=0, bytes_accessed=cost << 10, transcendentals=0),
        **options,
    )(*pinned)


def in_hbm(array):
    return pltpu.with_memory_space_constraint(array, pltpu.HBM)


PAIR = pltpu.VMEM((PIX, TICKS * GROUPS, LANES), bf16)
WIDE = pltpu.VMEM((PIX * TICKS * GROUPS, LANES), f32)
ROWS = pltpu.VMEM((PIX, C), f32)
PADDED = pltpu.VMEM((PAD_ROWS, LANES), f32)
DENSE = pltpu.VMEM((DENSE_ROWS, LANES), f32)
MIXED = pltpu.VMEM((PIX, C), bf16)
TILED = pltpu.VMEM((HW, HW, C), bf16)
IMAGE = jax.ShapeDtypeStruct((HW, HW, C), bf16)
MESSAGE = jax.ShapeDtypeStruct((PIX, C), bf16)


def sems(count):
    return pltpu.SemaphoreType.DMA((count,)) if count > 1 else pltpu.SemaphoreType.DMA


def pair_view(array):
    moved = jnp.transpose(array, (1, 2, 0, 3)).reshape(HW, HW, TICKS, GROUPS, LANES)
    return jnp.transpose(moved, (0, 1, 3, 2, 4)).reshape(PIX, TICKS * GROUPS, LANES)


def shifted(value, by):
    peers = lax.axis_size("section")
    pairs = [(i, i + by) for i in range(peers) if 0 <= i + by < peers]
    return lax.ppermute(value, "section", pairs)


def other_core(value):
    return lax.ppermute(value, "dp", [(0, 1), (1, 0), (2, 3), (3, 2)])


def other_chip(value):
    return lax.ppermute(value, "dp", [(0, 2), (2, 0), (1, 3), (3, 1)])


def per_device(activations, incoming, saved, images, head_grads, pw_weight, dw_kernel):
    weight = pw_weight[0]
    taps = dw_kernel[0].reshape(TAPS, GROUPS, LANES)
    saved_pair = pair_view(saved[:, 0, 0, 0])
    image_pair = pair_view(images[:, 0, 0])
    head_pair = pair_view(head_grads[:, 0, 0])

    out0, w, t = call(
        forward_first,
        [HBM] * 3,
        (MESSAGE, jax.ShapeDtypeStruct((C, C), bf16), jax.ShapeDtypeStruct((TAPS, GROUPS, LANES), f32)),
        [TILED, ROWS, PADDED, DENSE, MIXED, sems(3)],
        (activations[0, 0, 0], weight, taps),
    )
    act1 = shifted(out0, 1)
    grad_in0, g0 = call(
        backward_first,
        [HBM] * 2 + [VMEM, VMEM, ANY],
        (MESSAGE, MESSAGE),
        [TILED, ROWS, PADDED, DENSE, DENSE, PAIR, WIDE, sems(2)],
        (incoming[0, 0, 0], saved_pair, w, t, out0),
    )
    g1 = shifted(grad_in0, -1)
    keep, send, keep_rect = call(
        factors_kernel,
        [HBM, VMEM, ANY],
        (MESSAGE, jax.ShapeDtypeStruct((PIX, 2 * C), bf16), MESSAGE),
        [ROWS, PADDED, DENSE, PAIR, WIDE, sems(1)],
        (saved_pair, t, grad_in0),
    )
    peer = other_core(send)
    g0_peer = other_core(g0)

    out1 = call(
        forward_second,
        [VMEM] * 3 + [HBM, ANY],
        MESSAGE,
        [ROWS, PADDED, DENSE, MIXED, PAIR, WIDE, sems(1)],
        (act1, w, t, image_pair, keep),
        8192,
    )
    act2 = shifted(out1, 1)
    g1, _ = lax.optimization_barrier((g1, out1))
    g1 = call(
        head_kernel,
        [ANY, HBM],
        MESSAGE,
        [PAIR, WIDE, MIXED, sems(1)],
        (g1, head_pair),
        outs=ANY,
        input_output_aliases={0: 0},
    )
    g1_peer = other_core(g1)
    total = call(
        weight_first,
        [VMEM] * 4,
        jax.ShapeDtypeStruct((HALF, C), f32),
        [],
        (keep, g0, peer, g0_peer),
    )
    own, other = call(
        weight_second,
        [VMEM] * 5,
        (jax.ShapeDtypeStruct((QUARTER, C), f32), jax.ShapeDtypeStruct((QUARTER, C), bf16)),
        [],
        (total, keep, g1, peer, g1_peer),
    )
    arrived = other_chip(other)
    grad_in1 = call(
        backward_second,
        [VMEM, HBM, VMEM, VMEM, ANY],
        MESSAGE,
        [ROWS, PADDED, DENSE, DENSE, PAIR, WIDE, sems(1)],
        (g1, saved_pair, w, t, other),
    )
    g2 = shifted(grad_in1, -1)

    act_out = call(
        functools.partial(unpack_kernel, is_first),
        [VMEM, HBM],
        IMAGE,
        [ROWS, PAIR, WIDE, sems(1)],
        (act2, image_pair),
    )
    own_k, far_k = call(
        taps_kernel,
        [VMEM] * 7 + [HBM],
        (jax.ShapeDtypeStruct((TAPS, QUARTER), f32), jax.ShapeDtypeStruct((TAPS, QUARTER), bf16)),
        [PADDED, PADDED, pltpu.VMEM((32, HALF), f32)],
        (keep_rect, peer, g0, g0_peer, g1, g1_peer, w, act_out),
    )
    scale = 1.0 / (lax.axis_size("dp") * TICKS)
    k_grad = (own_k + other_chip(far_k).astype(f32)) * scale
    grad_out = call(
        functools.partial(unpack_kernel, is_last),
        [VMEM, HBM],
        IMAGE,
        [ROWS, PAIR, WIDE, sems(1)],
        (g2, head_pair),
    )
    w_grad = call(
        final_kernel, [VMEM, VMEM], jax.ShapeDtypeStruct((QUARTER, C), f32), [], (own, arrived)
    )
    return (act_out[None, None, None], grad_out[None, None, None], w_grad[None], k_grad[None])


def solution(mesh):
    in_specs = (
        P("section", "dp", None, None, None, None),
        P("section", "dp", None, None, None, None),
        P(None, "section", "dp", None, None, None, None),
        P(None, "dp", None, None, None, None),
        P(None, "dp", None, None, None, None),
        P("section", None, None),
        P("section", None, None),
    )
    out_specs = (
        P("section", "dp", None, None, None, None),
        P("section", "dp", None, None, None, None),
        P("section", "dp", None),
        P("section", None, "dp"),
    )
    return jax.shard_map(
        per_device, mesh=mesh, in_specs=in_specs, out_specs=out_specs, check_vma=False
    )
```

```python
import functools

import jax
import jax.numpy as jnp
from jax import lax
from jax.experimental import pallas as pl
from jax.experimental.pallas import tpu as pltpu
from jax.sharding import PartitionSpec as P

KW = 5
TAPS = KW * KW
TICKS = 2
HW = 14
PIX = HW * HW
C = 1024
LANES = 128
GROUPS = C // LANES
ROW = HW * GROUPS
HALF = C // 2
QUARTER = C // 4
PAD_ROWS = (HW + KW - 1) * ROW
DENSE_ROWS = PIX * GROUPS
TOP = (KW // 2) * ROW

f32 = jnp.float32
bf16 = jnp.bfloat16


def cols(group):
    return slice(group * LANES, (group + 1) * LANES)


def zero_pad(spread):
    zeros = jnp.zeros((TOP, LANES), f32)
    spread[0:TOP, :] = zeros
    spread[PAD_ROWS - TOP : PAD_ROWS, :] = zeros


def tile_at(spread, pixel):
    return spread[pl.ds(pl.multiple_of(pixel * GROUPS, GROUPS), GROUPS), :]


def conv(padded, taps, emit, flip):
    def row(p, carry):
        acc = [None] * HW
        for a in range(KW):
            tiles = [tile_at(padded, (p + a) * HW + q) for q in range(HW)]
            for b in range(KW):
                index = KW * a + b
                tap = taps[TAPS - 1 - index if flip else index]
                for q in range(HW):
                    src = q + b - KW // 2
                    if 0 <= src < HW:
                        term = tiles[src] * tap
                        acc[q] = term if acc[q] is None else acc[q] + term
        for q in range(HW):
            emit(p * HW + q, acc[q])
        return carry

    lax.fori_loop(0, HW, row, 0)


def tap_sums(rect_padded, grad_padded):
    def row(p, acc):
        acc = list(acc)
        grads = [tile_at(grad_padded, (p + KW // 2) * HW + q) for q in range(HW)]
        for a in range(KW):
            tiles = [tile_at(rect_padded, (p + a) * HW + q) for q in range(HW)]
            for b in range(KW):
                index = KW * a + b
                for q in range(HW):
                    src = q + b - KW // 2
                    if 0 <= src < HW:
                        acc[index] = acc[index] + tiles[src] * grads[q]
        return tuple(acc)

    return lax.fori_loop(0, HW, row, (jnp.zeros((GROUPS, LANES), f32),) * TAPS)


def store_tile(dense):
    def emit(pixel, value):
        dense[pl.ds(pl.multiple_of(pixel * GROUPS, GROUPS), GROUPS), :] = value

    return emit


def spread_rows(padded, group, value):
    padded[pl.ds(TOP + group, PIX, stride=GROUPS), :] = value


def rows_of(dense, group):
    return dense[pl.ds(group, PIX, stride=GROUPS), :]


def pack_rows(image, dst):
    for p in range(HW):
        dst[p * HW : (p + 1) * HW, :] = image[p].astype(f32)


def widen_pair(pair, wide):
    def step(p, carry):
        wide[pl.ds(pl.multiple_of(p * HW * 16, 16), HW * 16), :] = (
            pair[pl.ds(p * HW, HW)].astype(f32).reshape(HW * 16, LANES)
        )
        return carry

    lax.fori_loop(0, HW, step, 0)


def pair_tick_spread(wide, tick):
    return wide[pl.ds(tick, DENSE_ROWS, stride=TICKS), :]


def pair_tick_rows(wide, tick, group):
    return wide[pl.ds(tick + TICKS * group, PIX, stride=TICKS * GROUPS), :]


def replace_at_edge(edge, pair_hbm, tick, pair, wide, rows, sem):
    @pl.when(edge)
    def _():
        fetch(pair_hbm, pair, sem)
        widen_pair(pair, wide)
        for group in range(GROUPS):
            rows[:, cols(group)] = pair_tick_rows(wide, tick, group).astype(rows.dtype)


def fetch(src, dst, sem):
    copy = pltpu.make_async_copy(src, dst, sem)
    copy.start()
    copy.wait()


def is_first():
    return lax.axis_index("section") == 0


def is_last():
    return lax.axis_index("section") == lax.axis_size("section") - 1


def mix(rows, padded, dense, mixed, taps):
    zero_pad(padded)
    for group in range(GROUPS):
        spread_rows(padded, group, jnp.maximum(rows[:, cols(group)], 0.0))
    conv(padded, taps, store_tile(dense), False)
    for group in range(GROUPS):
        mixed[:, cols(group)] = rows_of(dense, group).astype(bf16)


def forward_first(x_hbm, weight, taps, token, out, x, rows, padded, dense, mixed, sem):
    fetch(x_hbm, x, sem)
    pack_rows(x, rows)
    mix(rows, padded, dense, mixed, taps)
    out[...] = (rows[...] + jnp.dot(mixed[...], weight[...], preferred_element_type=f32)).astype(bf16)


def forward_second(x, weight, taps, images, token, out, rows, padded, dense, mixed, pair, wide, sem):
    rows[...] = x[...].astype(f32)
    replace_at_edge(is_first(), images, 0, pair, wide, rows, sem)
    mix(rows, padded, dense, mixed, taps)
    out[...] = (rows[...] + jnp.dot(mixed[...], weight[...], preferred_element_type=f32)).astype(bf16)


def head_kernel(g_in, heads, token, g_out, pair, wide, rows, sem):
    @pl.when(is_last())
    def _():
        fetch(heads, pair, sem)
        widen_pair(pair, wide)
        for group in range(GROUPS):
            rows[:, cols(group)] = pair_tick_rows(wide, 0, group).astype(bf16)
        fetch(rows, g_out, sem)


def spread_grad(g, weight, grad_mixed):
    product = lax.dot_general(
        g[...], weight[...], (((1,), (1,)), ((), ())), preferred_element_type=f32
    )
    zero_pad(grad_mixed)
    for group in range(GROUPS):
        spread_rows(grad_mixed, group, product[:, cols(group)])


def finish_backward(tick, taps, wide, out, grad_mixed, rows, dense, mask):
    mask[...] = pair_tick_spread(wide, tick)

    def emit(pixel, value):
        keep = tile_at(mask, pixel) > 0.0
        store_tile(dense)(pixel, jnp.where(keep, value, 0.0))

    conv(grad_mixed, taps, emit, True)
    for group in range(GROUPS):
        out[:, cols(group)] = (rows[:, cols(group)] + rows_of(dense, group)).astype(bf16)


def backward_first(
    g_hbm, saved, w_hbm, taps_hbm, out, g_rows, weight, taps, g, rows, grad_mixed, dense, mask, pair, wide, sems
):
    copies = [
        pltpu.make_async_copy(src, dst, sems.at[i])
        for i, (src, dst) in enumerate(
            [(g_hbm, g), (w_hbm, weight), (saved, pair), (taps_hbm, taps)]
        )
    ]
    for copy in copies:
        copy.start()
    copies[0].wait()
    pack_rows(g, rows)
    g_rows[...] = rows[...].astype(bf16)
    copies[1].wait()
    spread_grad(g_rows, weight, grad_mixed)
    copies[2].wait()
    widen_pair(pair, wide)
    copies[3].wait()
    finish_backward(0, taps, wide, out, grad_mixed, rows, dense, mask)


def backward_second(
    g, saved, weight, taps, token, out, rows, grad_mixed, dense, mask, pair, wide, sem
):
    copy = pltpu.make_async_copy(saved, pair, sem)
    copy.start()
    rows[...] = g[...].astype(f32)
    spread_grad(g, weight, grad_mixed)
    copy.wait()
    widen_pair(pair, wide)
    finish_backward(1, taps, wide, out, grad_mixed, rows, dense, mask)


def halves(core):
    return [2 * core, 2 * core + 1, 4 + 2 * core, 5 + 2 * core]


def factors_kernel(saved, taps, token, keep, send, keep_rect, rows, padded, dense, pair, wide, sem):
    core = lax.rem(lax.axis_index("dp"), 2)
    high = lax.div(lax.axis_index("dp"), 2)
    fetch(saved, pair, sem)
    widen_pair(pair, wide)
    zero_pad(padded)
    for tick in range(TICKS):
        padded[TOP : TOP + DENSE_ROWS, :] = jnp.maximum(pair_tick_spread(wide, tick), 0.0)
        for at, (mine, theirs) in enumerate(zip(halves(core), halves(1 - core))):
            place = tick * HALF + at * LANES
            keep_rect[:, place : place + LANES] = rows_of(padded, TOP + mine).astype(bf16)
            send[:, C + place : C + place + LANES] = rows_of(padded, TOP + theirs).astype(bf16)
        conv(padded, taps, store_tile(dense), False)
        for group in range(GROUPS):
            rows[:, cols(group)] = rows_of(dense, group)
        for place in range(2):
            side = high if place == 0 else 1 - high
            at = tick * HALF + place * QUARTER
            own = pl.multiple_of((side * 2 + core) * QUARTER, QUARTER)
            other = pl.multiple_of((side * 2 + 1 - core) * QUARTER, QUARTER)
            keep[:, at : at + QUARTER] = rows[:, pl.ds(own, QUARTER)].astype(bf16)
            send[:, at : at + QUARTER] = rows[:, pl.ds(other, QUARTER)].astype(bf16)


def weight_term(factor, grads):
    return lax.dot_general(factor, grads, (((0,), (0,)), ((), ())), preferred_element_type=f32)


def weight_first(keep, g_own, peer, g_peer, out):
    out[...] = weight_term(keep[:, :HALF], g_own[...])
    out[...] += weight_term(peer[:, :HALF], g_peer[...])


def weight_second(total, keep, g_own, peer, g_peer, own, other):
    for place in range(2):
        rows = slice(place * QUARTER, (place + 1) * QUARTER)
        part = slice(HALF + place * QUARTER, HALF + (place + 1) * QUARTER)
        value = total[rows, :] + weight_term(keep[:, part], g_own[...])
        value += weight_term(peer[:, part], g_peer[...])
        if place == 0:
            own[...] = value
        else:
            other[...] = value.astype(bf16)


def taps_kernel(keep_rect, peer, g0, g0_peer, g1, g1_peer, weight, token, own, far, rect, grad, sums):
    core = lax.rem(lax.axis_index("dp"), 2)
    high = lax.div(lax.axis_index("dp"), 2)
    zero_pad(rect)
    zero_pad(grad)
    sums[...] = jnp.zeros_like(sums)
    for tick in range(TICKS):
        grads = (g0, g1)[tick][...], (g0_peer, g1_peer)[tick][...]
        for image in range(2):
            for side in range(2):
                rows = weight[pl.ds(pl.multiple_of((2 * side + core) * QUARTER, QUARTER), QUARTER), :]
                product = lax.dot_general(
                    grads[image], rows, (((1,), (1,)), ((), ())), preferred_element_type=f32
                )
                for part in range(2):
                    at = 2 * side + part
                    spread_rows(grad, 4 * image + at, product[:, cols(part)])
                    place = tick * HALF + at * LANES
                    source = keep_rect if image == 0 else peer
                    place += 0 if image == 0 else C
                    spread_rows(rect, 4 * image + at, source[:, place : place + LANES].astype(f32))
        terms = tap_sums(rect, grad)
        for index in range(TAPS):
            both = terms[index][0:4] + terms[index][4:8]
            sums[index : index + 1, :HALF] += jnp.concatenate(
                [both[i : i + 1] for i in range(4)], axis=1
            )
    low, top = sums[0:TAPS, 0:QUARTER], sums[0:TAPS, QUARTER:HALF]
    own[...] = jnp.where(high == 0, low, top)
    far[...] = jnp.where(high == 0, top, low).astype(bf16)


def final_kernel(own, arrived, out):
    out[...] = (own[...] + arrived[...].astype(f32)) * (1.0 / (2 * 2 * TICKS))


def unpack_kernel(edge, message, images, out, rows, pair, wide, sem):
    rows[...] = message[...].astype(f32)
    replace_at_edge(edge(), images, 1, pair, wide, rows, sem)
    for p in range(HW):
        out[p] = rows[p * HW : (p + 1) * HW, :].astype(bf16)


VMEM = pl.BlockSpec(memory_space=pltpu.VMEM)
HBM = pl.BlockSpec(memory_space=pltpu.HBM)
ANY = pl.BlockSpec(memory_space=pl.ANY)


def call(kernel, ins, out_shape, scratch, args, cost=1, outs=None, **options):
    pinned = [in_hbm(arg) if spec is HBM else arg for spec, arg in zip(ins, args)]
    return pl.pallas_call(
        kernel,
        in_specs=ins,
        out_specs=jax.tree.map(lambda _: VMEM, out_shape) if outs is None else outs,
        out_shape=out_shape,
        scratch_shapes=scratch,
        compiler_params=pltpu.CompilerParams(vmem_limit_bytes=20 * 1024 * 1024),
        cost_estimate=pl.CostEstimate(flops=0, bytes_accessed=cost << 10, transcendentals=0),
        **options,
    )(*pinned)


def in_hbm(array):
    return pltpu.with_memory_space_constraint(array, pltpu.HBM)


PAIR = pltpu.VMEM((PIX, TICKS * GROUPS, LANES), bf16)
WIDE = pltpu.VMEM((PIX * TICKS * GROUPS, LANES), f32)
ROWS = pltpu.VMEM((PIX, C), f32)
PADDED = pltpu.VMEM((PAD_ROWS, LANES), f32)
DENSE = pltpu.VMEM((DENSE_ROWS, LANES), f32)
MIXED = pltpu.VMEM((PIX, C), bf16)
TILED = pltpu.VMEM((HW, HW, C), bf16)
IMAGE = jax.ShapeDtypeStruct((HW, HW, C), bf16)
MESSAGE = jax.ShapeDtypeStruct((PIX, C), bf16)


def sems(count):
    return pltpu.SemaphoreType.DMA((count,)) if count > 1 else pltpu.SemaphoreType.DMA


def pair_view(array):
    moved = jnp.transpose(array, (1, 2, 0, 3)).reshape(HW, HW, TICKS, GROUPS, LANES)
    return jnp.transpose(moved, (0, 1, 3, 2, 4)).reshape(PIX, TICKS * GROUPS, LANES)


def shifted(value, by):
    peers = lax.axis_size("section")
    pairs = [(i, i + by) for i in range(peers) if 0 <= i + by < peers]
    return lax.ppermute(value, "section", pairs)


def other_core(value):
    return lax.ppermute(value, "dp", [(0, 1), (1, 0), (2, 3), (3, 2)])


def other_chip(value):
    return lax.ppermute(value, "dp", [(0, 2), (2, 0), (1, 3), (3, 1)])


def per_device(activations, incoming, saved, images, head_grads, pw_weight, dw_kernel):
    weight = pw_weight[0]
    taps = dw_kernel[0].reshape(TAPS, GROUPS, LANES)
    saved_pair = pair_view(saved[:, 0, 0, 0])
    image_pair = pair_view(images[:, 0, 0])
    head_pair = pair_view(head_grads[:, 0, 0])

    grad_in0, g0, w, t = call(
        backward_first,
        [HBM] * 4,
        (
            MESSAGE,
            MESSAGE,
            jax.ShapeDtypeStruct((C, C), bf16),
            jax.ShapeDtypeStruct((TAPS, GROUPS, LANES), f32),
        ),
        [TILED, ROWS, PADDED, DENSE, DENSE, PAIR, WIDE, sems(4)],
        (incoming[0, 0, 0], saved_pair, weight, taps),
    )
    g1 = shifted(grad_in0, -1)
    out0 = call(
        forward_first,
        [HBM, VMEM, VMEM, ANY],
        MESSAGE,
        [TILED, ROWS, PADDED, DENSE, MIXED, sems(1)],
        (activations[0, 0, 0], w, t, grad_in0),
    )
    act1 = shifted(out0, 1)
    keep, send, keep_rect = call(
        factors_kernel,
        [HBM, VMEM, ANY],
        (MESSAGE, jax.ShapeDtypeStruct((PIX, 2 * C), bf16), MESSAGE),
        [ROWS, PADDED, DENSE, PAIR, WIDE, sems(1)],
        (saved_pair, t, out0),
    )
    peer = other_core(send)
    g0_peer = other_core(g0)

    g1 = call(
        head_kernel,
        [ANY, HBM, ANY],
        MESSAGE,
        [PAIR, WIDE, MIXED, sems(1)],
        (g1, head_pair, act1),
        outs=ANY,
        input_output_aliases={0: 0},
    )
    g1_peer = other_core(g1)
    total = call(
        weight_first,
        [VMEM] * 4,
        jax.ShapeDtypeStruct((HALF, C), f32),
        [],
        (keep, g0, peer, g0_peer),
    )
    own, other = call(
        weight_second,
        [VMEM] * 5,
        (jax.ShapeDtypeStruct((QUARTER, C), f32), jax.ShapeDtypeStruct((QUARTER, C), bf16)),
        [],
        (total, keep, g1, peer, g1_peer),
    )
    arrived = other_chip(other)
    out1 = call(
        forward_second,
        [VMEM] * 3 + [HBM, ANY],
        MESSAGE,
        [ROWS, PADDED, DENSE, MIXED, PAIR, WIDE, sems(1)],
        (act1, w, t, image_pair, other),
    )
    act2 = shifted(out1, 1)
    grad_in1 = call(
        backward_second,
        [VMEM, HBM, VMEM, VMEM, ANY],
        MESSAGE,
        [ROWS, PADDED, DENSE, DENSE, PAIR, WIDE, sems(1)],
        (g1, saved_pair, w, t, out1),
    )
    g2 = shifted(grad_in1, -1)

    act_out = call(
        functools.partial(unpack_kernel, is_first),
        [VMEM, HBM],
        IMAGE,
        [ROWS, PAIR, WIDE, sems(1)],
        (act2, image_pair),
    )
    own_k, far_k = call(
        taps_kernel,
        [VMEM] * 7 + [ANY],
        (jax.ShapeDtypeStruct((TAPS, QUARTER), f32), jax.ShapeDtypeStruct((TAPS, QUARTER), bf16)),
        [PADDED, PADDED, pltpu.VMEM((32, HALF), f32)],
        (keep_rect, peer, g0, g0_peer, g1, g1_peer, w, grad_in1),
    )
    scale = 1.0 / (lax.axis_size("dp") * TICKS)
    k_grad = (own_k + other_chip(far_k).astype(f32)) * scale
    grad_out = call(
        functools.partial(unpack_kernel, is_last),
        [VMEM, HBM],
        IMAGE,
        [ROWS, PAIR, WIDE, sems(1)],
        (g2, head_pair),
    )
    w_grad = call(
        final_kernel, [VMEM, VMEM], jax.ShapeDtypeStruct((QUARTER, C), f32), [], (own, arrived)
    )
    return (act_out[None, None, None], grad_out[None, None, None], w_grad[None], k_grad[None])


def solution(mesh):
    in_specs = (
        P("section", "dp", None, None, None, None),
        P("section", "dp", None, None, None, None),
        P(None, "section", "dp", None, None, None, None),
        P(None, "dp", None, None, None, None),
        P(None, "dp", None, None, None, None),
        P("section", None, None),
        P("section", None, None),
    )
    out_specs = (
        P("section", "dp", None, None, None, None),
        P("section", "dp", None, None, None, None),
        P("section", "dp", None),
        P("section", None, "dp"),
    )
    return jax.shard_map(
        per_device, mesh=mesh, in_specs=in_specs, out_specs=out_specs, check_vma=False
    )
```

```python
import functools

import jax
import jax.numpy as jnp
from jax import lax
from jax.experimental import pallas as pl
from jax.experimental.pallas import tpu as pltpu
from jax.sharding import PartitionSpec as P

KW = 5
TAPS = KW * KW
TICKS = 2
HW = 14
PIX = HW * HW
C = 1024
LANES = 128
GROUPS = C // LANES
ROW = HW * GROUPS
HALF = C // 2
QUARTER = C // 4
PAD_ROWS = (HW + KW - 1) * ROW
DENSE_ROWS = PIX * GROUPS
TOP = (KW // 2) * ROW

f32 = jnp.float32
bf16 = jnp.bfloat16


def cols(group):
    return slice(group * LANES, (group + 1) * LANES)


def zero_pad(spread):
    zeros = jnp.zeros((TOP, LANES), f32)
    spread[0:TOP, :] = zeros
    spread[PAD_ROWS - TOP : PAD_ROWS, :] = zeros


def tile_at(spread, pixel):
    return spread[pl.ds(pl.multiple_of(pixel * GROUPS, GROUPS), GROUPS), :]


def conv(padded, taps, emit, flip):
    def row(p, carry):
        acc = [None] * HW
        for a in range(KW):
            tiles = [tile_at(padded, (p + a) * HW + q) for q in range(HW)]
            for b in range(KW):
                index = KW * a + b
                tap = taps[TAPS - 1 - index if flip else index]
                for q in range(HW):
                    src = q + b - KW // 2
                    if 0 <= src < HW:
                        term = tiles[src] * tap
                        acc[q] = term if acc[q] is None else acc[q] + term
        for q in range(HW):
            emit(p * HW + q, acc[q])
        return carry

    lax.fori_loop(0, HW, row, 0)


def tap_sums(rect_padded, grad_padded):
    def row(p, acc):
        acc = list(acc)
        grads = [tile_at(grad_padded, (p + KW // 2) * HW + q) for q in range(HW)]
        for a in range(KW):
            tiles = [tile_at(rect_padded, (p + a) * HW + q) for q in range(HW)]
            for b in range(KW):
                index = KW * a + b
                for q in range(HW):
                    src = q + b - KW // 2
                    if 0 <= src < HW:
                        acc[index] = acc[index] + tiles[src] * grads[q]
        return tuple(acc)

    return lax.fori_loop(0, HW, row, (jnp.zeros((GROUPS, LANES), f32),) * TAPS)


def store_tile(dense):
    def emit(pixel, value):
        dense[pl.ds(pl.multiple_of(pixel * GROUPS, GROUPS), GROUPS), :] = value

    return emit


def spread_rows(padded, group, value):
    padded[pl.ds(TOP + group, PIX, stride=GROUPS), :] = value


def rows_of(dense, group):
    return dense[pl.ds(group, PIX, stride=GROUPS), :]


def pack_rows(image, dst):
    for p in range(HW):
        dst[p * HW : (p + 1) * HW, :] = image[p].astype(f32)


def widen_pair(pair, wide):
    def step(p, carry):
        wide[pl.ds(pl.multiple_of(p * HW * 16, 16), HW * 16), :] = (
            pair[pl.ds(p * HW, HW)].astype(f32).reshape(HW * 16, LANES)
        )
        return carry

    lax.fori_loop(0, HW, step, 0)


def pair_tick_spread(wide, tick):
    return wide[pl.ds(tick, DENSE_ROWS, stride=TICKS), :]


def pair_tick_rows(wide, tick, group):
    return wide[pl.ds(tick + TICKS * group, PIX, stride=TICKS * GROUPS), :]


def replace_at_edge(edge, pair_hbm, tick, pair, wide, rows, sem):
    @pl.when(edge)
    def _():
        fetch(pair_hbm, pair, sem)
        widen_pair(pair, wide)
        for group in range(GROUPS):
            rows[:, cols(group)] = pair_tick_rows(wide, tick, group).astype(rows.dtype)


def fetch(src, dst, sem):
    copy = pltpu.make_async_copy(src, dst, sem)
    copy.start()
    copy.wait()


def is_first():
    return lax.axis_index("section") == 0


def is_last():
    return lax.axis_index("section") == lax.axis_size("section") - 1


def mix(rows, padded, dense, mixed, taps):
    zero_pad(padded)
    for group in range(GROUPS):
        spread_rows(padded, group, jnp.maximum(rows[:, cols(group)], 0.0))
    conv(padded, taps, store_tile(dense), False)
    for group in range(GROUPS):
        mixed[:, cols(group)] = rows_of(dense, group).astype(bf16)


def forward_first(x, weight, taps, token, out, rows, padded, dense, mixed):
    pack_rows(x, rows)
    mix(rows, padded, dense, mixed, taps)
    out[...] = (rows[...] + jnp.dot(mixed[...], weight[...], preferred_element_type=f32)).astype(bf16)


def forward_second(x, weight, taps, images, token, out, rows, padded, dense, mixed, pair, wide, sem):
    rows[...] = x[...].astype(f32)
    replace_at_edge(is_first(), images, 0, pair, wide, rows, sem)
    mix(rows, padded, dense, mixed, taps)
    out[...] = (rows[...] + jnp.dot(mixed[...], weight[...], preferred_element_type=f32)).astype(bf16)


def head_kernel(g_in, heads, token, g_out, pair, wide, rows, sem):
    @pl.when(is_last())
    def _():
        fetch(heads, pair, sem)
        widen_pair(pair, wide)
        for group in range(GROUPS):
            rows[:, cols(group)] = pair_tick_rows(wide, 0, group).astype(bf16)
        fetch(rows, g_out, sem)


def spread_grad(g, weight, grad_mixed, waits=()):
    zero_pad(grad_mixed)
    for block in range(4):
        if waits:
            waits[block].wait()
        product = lax.dot_general(
            g[...],
            weight[block * QUARTER : (block + 1) * QUARTER, :],
            (((1,), (1,)), ((), ())),
            preferred_element_type=f32,
        )
        for part in range(2):
            spread_rows(grad_mixed, 2 * block + part, product[:, cols(part)])


def finish_backward(taps, out, grad_mixed, rows, dense, mask):
    def emit(pixel, value):
        keep = tile_at(mask, pixel) > 0.0
        store_tile(dense)(pixel, jnp.where(keep, value, 0.0))

    conv(grad_mixed, taps, emit, True)
    for group in range(GROUPS):
        out[:, cols(group)] = (rows[:, cols(group)] + rows_of(dense, group)).astype(bf16)


def backward_first(
    g_hbm, saved, w_hbm, taps_hbm, x_hbm, out, g_rows, weight, taps, pair, x, g, rows, grad_mixed, dense, mask, wide, sems
):
    blocks = [slice(block * QUARTER, (block + 1) * QUARTER) for block in range(4)]
    pieces = [(g_hbm, g), (saved, pair)]
    pieces += [(w_hbm.at[rows_, :], weight.at[rows_, :]) for rows_ in blocks]
    pieces += [(taps_hbm, taps), (x_hbm, x)]
    copies = [
        pltpu.make_async_copy(src, dst, sems.at[i]) for i, (src, dst) in enumerate(pieces)
    ]
    for copy in copies:
        copy.start()
    copies[0].wait()
    pack_rows(g, rows)
    g_rows[...] = rows[...].astype(bf16)
    copies[1].wait()
    widen_pair(pair, wide)
    mask[...] = pair_tick_spread(wide, 0)
    spread_grad(g_rows, weight, grad_mixed, copies[2:6])
    copies[6].wait()
    finish_backward(taps, out, grad_mixed, rows, dense, mask)
    copies[7].wait()


def backward_second(g, pair, weight, taps, token, out, rows, grad_mixed, dense, mask, wide):
    widen_pair(pair, wide)
    mask[...] = pair_tick_spread(wide, 1)
    rows[...] = g[...].astype(f32)
    spread_grad(g, weight, grad_mixed)
    finish_backward(taps, out, grad_mixed, rows, dense, mask)


def factors_kernel(pair, g_rows, taps, token, keep, send, padded, dense, wide):
    core = lax.rem(lax.axis_index("dp"), 2)
    high = lax.div(lax.axis_index("dp"), 2)
    widen_pair(pair, wide)
    send[:, C : 2 * C] = g_rows[...]
    zero_pad(padded)
    for tick in range(TICKS):
        padded[TOP : TOP + DENSE_ROWS, :] = jnp.maximum(pair_tick_spread(wide, tick), 0.0)
        conv(padded, taps, store_tile(dense), False)
        for place in range(2):
            side = high if place == 0 else 1 - high
            for part in range(2):
                at = tick * HALF + (2 * place + part) * LANES
                mine = 4 * side + 2 * core + part
                theirs = 4 * side + 2 * (1 - core) + part
                keep[:, at : at + LANES] = rows_of(dense, mine).astype(bf16)
                send[:, at : at + LANES] = rows_of(dense, theirs).astype(bf16)


def weight_term(factor, grads):
    return lax.dot_general(factor, grads, (((0,), (0,)), ((), ())), preferred_element_type=f32)


def weight_first(keep, g_own, peer, out):
    out[...] = weight_term(keep[:, :HALF], g_own[...])
    out[...] += weight_term(peer[:, :HALF], peer[:, C : 2 * C])


def weight_second(total, keep, g_own, peer, g_peer, own, other):
    for place in range(2):
        rows = slice(place * QUARTER, (place + 1) * QUARTER)
        part = slice(HALF + place * QUARTER, HALF + (place + 1) * QUARTER)
        value = total[rows, :] + weight_term(keep[:, part], g_own[...])
        value += weight_term(peer[:, part], g_peer[...])
        if place == 0:
            own[...] = value
        else:
            other[...] = value.astype(bf16)


def taps_kernel(pair, g0, g1, weight, token, own, core_out, chip_out, both_out, rect, grad, sums, wide):
    core = lax.rem(lax.axis_index("dp"), 2)
    high = lax.div(lax.axis_index("dp"), 2)
    widen_pair(pair, wide)
    zero_pad(rect)
    for tick in range(TICKS):
        rect[TOP : TOP + DENSE_ROWS, :] = jnp.maximum(pair_tick_spread(wide, tick), 0.0)
        spread_grad((g0, g1)[tick], weight, grad)
        terms = tap_sums(rect, grad)
        for index in range(TAPS):
            row = jnp.concatenate([terms[index][i : i + 1] for i in range(GROUPS)], axis=1)
            if tick == 0:
                sums[index : index + 1, :] = row
            else:
                sums[index : index + 1, :] += row

    def block(side, which):
        at = pl.multiple_of((2 * side + which) * QUARTER, QUARTER)
        return sums[0:TAPS, pl.ds(at, QUARTER)]

    own[...] = block(high, core)
    core_out[...] = block(high, 1 - core).astype(bf16)
    chip_out[...] = block(1 - high, core).astype(bf16)
    both_out[...] = block(1 - high, 1 - core).astype(bf16)


def final_kernel(own, arrived, out):
    out[...] = (own[...] + arrived[...].astype(f32)) * (1.0 / (2 * 2 * TICKS))


def unpack_kernel(edge, message, images, out, rows, pair, wide, sem):
    rows[...] = message[...].astype(f32)
    replace_at_edge(edge(), images, 1, pair, wide, rows, sem)
    for p in range(HW):
        out[p] = rows[p * HW : (p + 1) * HW, :].astype(bf16)


VMEM = pl.BlockSpec(memory_space=pltpu.VMEM)
HBM = pl.BlockSpec(memory_space=pltpu.HBM)
ANY = pl.BlockSpec(memory_space=pl.ANY)


def call(kernel, ins, out_shape, scratch, args, cost=1, outs=None, **options):
    pinned = [in_hbm(arg) if spec is HBM else arg for spec, arg in zip(ins, args)]
    return pl.pallas_call(
        kernel,
        in_specs=ins,
        out_specs=jax.tree.map(lambda _: VMEM, out_shape) if outs is None else outs,
        out_shape=out_shape,
        scratch_shapes=scratch,
        compiler_params=pltpu.CompilerParams(vmem_limit_bytes=20 * 1024 * 1024),
        cost_estimate=pl.CostEstimate(flops=0, bytes_accessed=cost << 10, transcendentals=0),
        **options,
    )(*pinned)


def in_hbm(array):
    return pltpu.with_memory_space_constraint(array, pltpu.HBM)


PAIR = pltpu.VMEM((PIX, TICKS * GROUPS, LANES), bf16)
WIDE = pltpu.VMEM((PIX * TICKS * GROUPS, LANES), f32)
ROWS = pltpu.VMEM((PIX, C), f32)
PADDED = pltpu.VMEM((PAD_ROWS, LANES), f32)
DENSE = pltpu.VMEM((DENSE_ROWS, LANES), f32)
MIXED = pltpu.VMEM((PIX, C), bf16)
TILED = pltpu.VMEM((HW, HW, C), bf16)
IMAGE = jax.ShapeDtypeStruct((HW, HW, C), bf16)
MESSAGE = jax.ShapeDtypeStruct((PIX, C), bf16)


def sems(count):
    return pltpu.SemaphoreType.DMA((count,)) if count > 1 else pltpu.SemaphoreType.DMA


def pair_view(array):
    moved = jnp.transpose(array, (1, 2, 0, 3)).reshape(HW, HW, TICKS, GROUPS, LANES)
    return jnp.transpose(moved, (0, 1, 3, 2, 4)).reshape(PIX, TICKS * GROUPS, LANES)


def shifted(value, by):
    peers = lax.axis_size("section")
    pairs = [(i, i + by) for i in range(peers) if 0 <= i + by < peers]
    return lax.ppermute(value, "section", pairs)


def other_core(value):
    return lax.ppermute(value, "dp", [(0, 1), (1, 0), (2, 3), (3, 2)])


def other_chip(value):
    return lax.ppermute(value, "dp", [(0, 2), (2, 0), (1, 3), (3, 1)])


def other_both(value):
    return lax.ppermute(value, "dp", [(0, 3), (3, 0), (1, 2), (2, 1)])


def per_device(activations, incoming, saved, images, head_grads, pw_weight, dw_kernel):
    weight = pw_weight[0]
    taps = dw_kernel[0].reshape(TAPS, GROUPS, LANES)
    saved_pair = pair_view(saved[:, 0, 0, 0])
    image_pair = pair_view(images[:, 0, 0])
    head_pair = pair_view(head_grads[:, 0, 0])

    grad_in0, g0, w, t, pair, x0 = call(
        backward_first,
        [HBM] * 5,
        (MESSAGE, MESSAGE)
        + tuple(
            jax.ShapeDtypeStruct(shape, kind)
            for shape, kind in (
                ((C, C), bf16),
                ((TAPS, GROUPS, LANES), f32),
                (PAIR.shape, bf16),
                (TILED.shape, bf16),
            )
        ),
        [TILED, ROWS, PADDED, DENSE, DENSE, WIDE, sems(8)],
        (incoming[0, 0, 0], saved_pair, weight, taps, activations[0, 0, 0]),
    )
    g1 = shifted(grad_in0, -1)
    keep, send = call(
        factors_kernel,
        [VMEM, VMEM, VMEM, ANY],
        (MESSAGE, jax.ShapeDtypeStruct((PIX, 2 * C), bf16)),
        [PADDED, DENSE, WIDE],
        (pair, g0, t, grad_in0),
    )
    peer = other_core(send)
    out0 = call(
        forward_first,
        [VMEM, VMEM, VMEM, ANY],
        MESSAGE,
        [ROWS, PADDED, DENSE, MIXED],
        (x0, w, t, keep),
    )
    act1 = shifted(out0, 1)
    g1 = call(
        head_kernel,
        [ANY, HBM, ANY],
        MESSAGE,
        [PAIR, WIDE, MIXED, sems(1)],
        (g1, head_pair, out0),
        outs=ANY,
        input_output_aliases={0: 0},
    )
    g1_peer = other_core(g1)
    total = call(
        weight_first,
        [VMEM] * 3,
        jax.ShapeDtypeStruct((HALF, C), f32),
        [],
        (keep, g0, peer),
    )
    own, other = call(
        weight_second,
        [VMEM] * 5,
        (jax.ShapeDtypeStruct((QUARTER, C), f32), jax.ShapeDtypeStruct((QUARTER, C), bf16)),
        [],
        (total, keep, g1, peer, g1_peer),
    )
    arrived = other_chip(other)
    grad_in1 = call(
        backward_second,
        [VMEM, VMEM, VMEM, VMEM, ANY],
        MESSAGE,
        [ROWS, PADDED, DENSE, DENSE, WIDE],
        (g1, pair, w, t, other),
    )
    g2 = shifted(grad_in1, -1)
    out1 = call(
        forward_second,
        [VMEM] * 3 + [HBM, ANY],
        MESSAGE,
        [ROWS, PADDED, DENSE, MIXED, PAIR, WIDE, sems(1)],
        (act1, w, t, image_pair, grad_in1),
    )
    act2 = shifted(out1, 1)

    small = jax.ShapeDtypeStruct((TAPS, QUARTER), bf16)
    own_k, core_k, chip_k, both_k = call(
        taps_kernel,
        [VMEM] * 4 + [ANY],
        (jax.ShapeDtypeStruct((TAPS, QUARTER), f32), small, small, small),
        [PADDED, PADDED, pltpu.VMEM((32, C), f32), WIDE],
        (pair, g0, g1, w, out1),
    )
    scale = 1.0 / (lax.axis_size("dp") * TICKS)
    far_k = other_chip(chip_k).astype(f32) + other_both(both_k).astype(f32)
    k_grad = (own_k + other_core(core_k).astype(f32) + far_k) * scale
    act_out = call(
        functools.partial(unpack_kernel, is_first),
        [VMEM, HBM],
        IMAGE,
        [ROWS, PAIR, WIDE, sems(1)],
        (act2, image_pair),
    )
    grad_out = call(
        functools.partial(unpack_kernel, is_last),
        [VMEM, HBM],
        IMAGE,
        [ROWS, PAIR, WIDE, sems(1)],
        (g2, head_pair),
    )
    w_grad = call(
        final_kernel, [VMEM, VMEM], jax.ShapeDtypeStruct((QUARTER, C), f32), [], (own, arrived)
    )
    return (act_out[None, None, None], grad_out[None, None, None], w_grad[None], k_grad[None])


def solution(mesh):
    in_specs = (
        P("section", "dp", None, None, None, None),
        P("section", "dp", None, None, None, None),
        P(None, "section", "dp", None, None, None, None),
        P(None, "dp", None, None, None, None),
        P(None, "dp", None, None, None, None),
        P("section", None, None),
        P("section", None, None),
    )
    out_specs = (
        P("section", "dp", None, None, None, None),
        P("section", "dp", None, None, None, None),
        P("section", "dp", None),
        P("section", None, "dp"),
    )
    return jax.shard_map(
        per_device, mesh=mesh, in_specs=in_specs, out_specs=out_specs, check_vma=False
    )
```

```python
import functools

import jax
import jax.numpy as jnp
from jax import lax
from jax.experimental import pallas as pl
from jax.experimental.pallas import tpu as pltpu
from jax.sharding import PartitionSpec as P

KW = 5
TAPS = KW * KW
TICKS = 2
HW = 14
PIX = HW * HW
PIX_ROWS = -(-PIX // 8) * 8
C = 1024
LANES = 128
GROUPS = C // LANES
ROW = HW * GROUPS
HALF = C // 2
QUARTER = C // 4
PAD_ROWS = (HW + KW - 1) * ROW
DENSE_ROWS = PIX * GROUPS
TOP = (KW // 2) * ROW

f32 = jnp.float32
bf16 = jnp.bfloat16


def cols(group):
    return slice(group * LANES, (group + 1) * LANES)


def zero_pad(spread):
    zeros = jnp.zeros((TOP, LANES), f32)
    spread[0:TOP, :] = zeros
    spread[PAD_ROWS - TOP : PAD_ROWS, :] = zeros


def tile_at(spread, pixel):
    return spread[pl.ds(pl.multiple_of(pixel * GROUPS, GROUPS), GROUPS), :]


def conv(padded, taps, emit, flip):
    def row(p, carry):
        acc = [None] * HW
        for a in range(KW):
            tiles = [tile_at(padded, (p + a) * HW + q) for q in range(HW)]
            for b in range(KW):
                index = KW * a + b
                tap = taps[TAPS - 1 - index if flip else index]
                for q in range(HW):
                    src = q + b - KW // 2
                    if 0 <= src < HW:
                        term = tiles[src] * tap
                        acc[q] = term if acc[q] is None else acc[q] + term
        for q in range(HW):
            emit(p * HW + q, acc[q])
        return carry

    lax.fori_loop(0, HW, row, 0)


def tap_sums(rect_padded, grad_padded):
    def row(p, acc):
        acc = list(acc)
        grads = [tile_at(grad_padded, (p + KW // 2) * HW + q) for q in range(HW)]
        for a in range(KW):
            tiles = [tile_at(rect_padded, (p + a) * HW + q) for q in range(HW)]
            for b in range(KW):
                index = KW * a + b
                for q in range(HW):
                    src = q + b - KW // 2
                    if 0 <= src < HW:
                        acc[index] = acc[index] + tiles[src] * grads[q]
        return tuple(acc)

    return lax.fori_loop(0, HW, row, (jnp.zeros((GROUPS, LANES), f32),) * TAPS)


def store_tile(dense):
    def emit(pixel, value):
        dense[pl.ds(pl.multiple_of(pixel * GROUPS, GROUPS), GROUPS), :] = value

    return emit


def spread_rows(padded, group, value):
    padded[pl.ds(TOP + group, PIX, stride=GROUPS), :] = value


def rows_of(dense, group):
    return dense[pl.ds(group, PIX, stride=GROUPS), :]


def pack_rows(image, dst):
    for p in range(HW):
        dst[p * HW : (p + 1) * HW, :] = image[p].astype(f32)


def widen_pair(pair, wide):
    def step(p, carry):
        wide[pl.ds(pl.multiple_of(p * HW * 16, 16), HW * 16), :] = (
            pair[pl.ds(p * HW, HW)].astype(f32).reshape(HW * 16, LANES)
        )
        return carry

    lax.fori_loop(0, HW, step, 0)


def pair_tick_spread(wide, tick):
    return wide[pl.ds(tick, DENSE_ROWS, stride=TICKS), :]


def pair_tick_rows(wide, tick, group):
    return wide[pl.ds(tick + TICKS * group, PIX, stride=TICKS * GROUPS), :]


def replace_at_edge(edge, pair_hbm, tick, pair, wide, rows, sem):
    @pl.when(edge)
    def _():
        fetch(pair_hbm, pair, sem)
        widen_pair(pair, wide)
        for group in range(GROUPS):
            rows[:, cols(group)] = pair_tick_rows(wide, tick, group).astype(rows.dtype)


def fetch(src, dst, sem):
    copy = pltpu.make_async_copy(src, dst, sem)
    copy.start()
    copy.wait()


def is_first():
    return lax.axis_index("section") == 0


def is_last():
    return lax.axis_index("section") == lax.axis_size("section") - 1


def mix(rows, padded, dense, mixed, taps):
    zero_pad(padded)
    for group in range(GROUPS):
        spread_rows(padded, group, jnp.maximum(rows[:, cols(group)], 0.0))
    conv(padded, taps, store_tile(dense), False)
    for group in range(GROUPS):
        mixed[:, cols(group)] = rows_of(dense, group).astype(bf16)


def forward_first(x, weight, taps, token, out, rows, padded, dense, mixed):
    pack_rows(x, rows)
    mix(rows, padded, dense, mixed, taps)
    out[...] = (rows[...] + jnp.dot(mixed[...], weight[...], preferred_element_type=f32)).astype(bf16)


def forward_second(x, weight, taps, images, token, out, rows, padded, dense, mixed, pair, wide, sem):
    rows[...] = x[...].astype(f32)
    replace_at_edge(is_first(), images, 0, pair, wide, rows, sem)
    mix(rows, padded, dense, mixed, taps)
    out[...] = (rows[...] + jnp.dot(mixed[...], weight[...], preferred_element_type=f32)).astype(bf16)


def head_kernel(g_in, heads, token, g_out, pair, wide, rows, sem):
    @pl.when(is_last())
    def _():
        fetch(heads, pair, sem)
        widen_pair(pair, wide)
        for group in range(GROUPS):
            rows[:, cols(group)] = pair_tick_rows(wide, 0, group).astype(bf16)
        fetch(rows, g_out, sem)


def spread_grad(g, weight, grad_mixed, waits=()):
    zero_pad(grad_mixed)
    for block in range(4):
        if waits:
            waits[block].wait()
        product = lax.dot_general(
            g[...],
            weight[block * QUARTER : (block + 1) * QUARTER, :],
            (((1,), (1,)), ((), ())),
            preferred_element_type=f32,
        )
        for part in range(2):
            spread_rows(grad_mixed, 2 * block + part, product[:, cols(part)])


def finish_backward(taps, out, grad_mixed, rows, dense, mask):
    def emit(pixel, value):
        keep = tile_at(mask, pixel) > 0.0
        store_tile(dense)(pixel, jnp.where(keep, value, 0.0))

    conv(grad_mixed, taps, emit, True)
    for group in range(GROUPS):
        out[0:PIX, cols(group)] = (rows[:, cols(group)] + rows_of(dense, group)).astype(bf16)


def backward_first(
    g_hbm, saved, w_hbm, taps_hbm, x_hbm, out, g_rows, weight, taps, pair, x, g, rows, grad_mixed, dense, mask, wide, sems
):
    blocks = [slice(block * QUARTER, (block + 1) * QUARTER) for block in range(4)]
    pieces = [(g_hbm, g), (saved, pair)]
    pieces += [(w_hbm.at[rows_, :], weight.at[rows_, :]) for rows_ in blocks]
    pieces += [(taps_hbm, taps), (x_hbm, x)]
    copies = [
        pltpu.make_async_copy(src, dst, sems.at[i]) for i, (src, dst) in enumerate(pieces)
    ]
    for copy in copies:
        copy.start()
    copies[0].wait()
    pack_rows(g, rows)
    g_rows[...] = rows[...].astype(bf16)
    copies[1].wait()
    widen_pair(pair, wide)
    mask[...] = pair_tick_spread(wide, 0)
    spread_grad(g_rows, weight, grad_mixed, copies[2:6])
    copies[6].wait()
    finish_backward(taps, out, grad_mixed, rows, dense, mask)
    copies[7].wait()


def backward_second(g, pair, weight, taps, token, out, rows, grad_mixed, dense, mask, wide):
    widen_pair(pair, wide)
    mask[...] = pair_tick_spread(wide, 1)
    rows[...] = g[...].astype(f32)
    spread_grad(g, weight, grad_mixed)
    out[PIX:PIX_ROWS, :] = jnp.zeros((PIX_ROWS - PIX, C), bf16)
    finish_backward(taps, out, grad_mixed, rows, dense, mask)


def factors_kernel(pair, g_rows, taps, token, keep, send, padded, dense, wide):
    core = lax.rem(lax.axis_index("dp"), 2)
    high = lax.div(lax.axis_index("dp"), 2)
    widen_pair(pair, wide)
    send[:, C : 2 * C] = g_rows[...]
    zero_pad(padded)
    for tick in range(TICKS):
        padded[TOP : TOP + DENSE_ROWS, :] = jnp.maximum(pair_tick_spread(wide, tick), 0.0)
        conv(padded, taps, store_tile(dense), False)
        for place in range(2):
            side = high if place == 0 else 1 - high
            for part in range(2):
                at = tick * HALF + (2 * place + part) * LANES
                mine = 4 * side + 2 * core + part
                theirs = 4 * side + 2 * (1 - core) + part
                keep[:, at : at + LANES] = rows_of(dense, mine).astype(bf16)
                send[:, at : at + LANES] = rows_of(dense, theirs).astype(bf16)


def weight_term(factor, grads):
    return lax.dot_general(factor, grads, (((0,), (0,)), ((), ())), preferred_element_type=f32)


def weight_first(keep, g_own, peer, out):
    out[...] = weight_term(keep[:, :HALF], g_own[...])
    out[...] += weight_term(peer[:, :HALF], peer[:, C : 2 * C])


def weight_second(total, keep, g_own, peer, g_peer, own, other):
    for place in range(2):
        rows = slice(place * QUARTER, (place + 1) * QUARTER)
        part = slice(HALF + place * QUARTER, HALF + (place + 1) * QUARTER)
        value = total[rows, :] + weight_term(keep[:, part], g_own[...])
        value += weight_term(peer[:, part], g_peer[...])
        if place == 0:
            own[...] = value
        else:
            other[...] = value.astype(bf16)


def taps_kernel(pair, g0, g1, weight, token, own, core_out, chip_out, both_out, rect, grad, sums, wide):
    core = lax.rem(lax.axis_index("dp"), 2)
    high = lax.div(lax.axis_index("dp"), 2)
    widen_pair(pair, wide)
    zero_pad(rect)
    for tick in range(TICKS):
        rect[TOP : TOP + DENSE_ROWS, :] = jnp.maximum(pair_tick_spread(wide, tick), 0.0)
        spread_grad((g0, g1)[tick], weight, grad)
        terms = tap_sums(rect, grad)
        for index in range(TAPS):
            row = jnp.concatenate([terms[index][i : i + 1] for i in range(GROUPS)], axis=1)
            if tick == 0:
                sums[index : index + 1, :] = row
            else:
                sums[index : index + 1, :] += row

    def block(side, which):
        at = pl.multiple_of((2 * side + which) * QUARTER, QUARTER)
        return sums[0:TAPS, pl.ds(at, QUARTER)]

    own[...] = block(high, core)
    core_out[...] = block(high, 1 - core).astype(bf16)
    chip_out[...] = block(1 - high, core).astype(bf16)
    both_out[...] = block(1 - high, 1 - core).astype(bf16)


SCALE = 1.0 / (2 * 2 * TICKS)


def final_kernel(own, arrived, out):
    out[...] = (own[...] + arrived[...].astype(f32)) * SCALE


def taps_final(own, from_core, from_chip, from_both, out):
    total = own[...] + from_core[...].astype(f32) + from_chip[...].astype(f32)
    total = (total + from_both[...].astype(f32)) * SCALE
    for part in range(2):
        out[:, part, :] = total[:, cols(part)]


def unpack_kernel(edge, message, images, token, out, packed, rows, pair, wide, sem):
    fetch(message, packed, sem)
    rows[...] = packed[0:PIX, :].astype(f32)
    replace_at_edge(edge(), images, 1, pair, wide, rows, sem)
    for p in range(HW):
        out[p] = rows[p * HW : (p + 1) * HW, :].astype(bf16)


VMEM = pl.BlockSpec(memory_space=pltpu.VMEM)
HBM = pl.BlockSpec(memory_space=pltpu.HBM)
ANY = pl.BlockSpec(memory_space=pl.ANY)


def call(kernel, ins, out_shape, scratch, args, cost=1, outs=None, **options):
    pinned = [in_hbm(arg) if spec is HBM else arg for spec, arg in zip(ins, args)]
    return pl.pallas_call(
        kernel,
        in_specs=ins,
        out_specs=jax.tree.map(lambda _: VMEM, out_shape) if outs is None else outs,
        out_shape=out_shape,
        scratch_shapes=scratch,
        compiler_params=pltpu.CompilerParams(vmem_limit_bytes=20 * 1024 * 1024),
        cost_estimate=pl.CostEstimate(flops=0, bytes_accessed=cost << 10, transcendentals=0),
        **options,
    )(*pinned)


def in_hbm(array):
    return pltpu.with_memory_space_constraint(array, pltpu.HBM)


PAIR = pltpu.VMEM((PIX, TICKS * GROUPS, LANES), bf16)
WIDE = pltpu.VMEM((PIX * TICKS * GROUPS, LANES), f32)
ROWS = pltpu.VMEM((PIX, C), f32)
PADDED = pltpu.VMEM((PAD_ROWS, LANES), f32)
DENSE = pltpu.VMEM((DENSE_ROWS, LANES), f32)
MIXED = pltpu.VMEM((PIX, C), bf16)
TILED = pltpu.VMEM((HW, HW, C), bf16)
IMAGE = jax.ShapeDtypeStruct((HW, HW, C), bf16)
MESSAGE = jax.ShapeDtypeStruct((PIX, C), bf16)
LONGER = jax.ShapeDtypeStruct((PIX_ROWS, C), bf16)


def sems(count):
    return pltpu.SemaphoreType.DMA((count,)) if count > 1 else pltpu.SemaphoreType.DMA


def pair_view(array):
    moved = jnp.transpose(array, (1, 2, 0, 3)).reshape(HW, HW, TICKS, GROUPS, LANES)
    return jnp.transpose(moved, (0, 1, 3, 2, 4)).reshape(PIX, TICKS * GROUPS, LANES)


def shifted(value, by):
    peers = lax.axis_size("section")
    pairs = [(i, i + by) for i in range(peers) if 0 <= i + by < peers]
    return lax.ppermute(value, "section", pairs)


def other_core(value):
    return lax.ppermute(value, "dp", [(0, 1), (1, 0), (2, 3), (3, 2)])


def other_chip(value):
    return lax.ppermute(value, "dp", [(0, 2), (2, 0), (1, 3), (3, 1)])


def other_both(value):
    return lax.ppermute(value, "dp", [(0, 3), (3, 0), (1, 2), (2, 1)])


def per_device(activations, incoming, saved, images, head_grads, pw_weight, dw_kernel):
    weight = pw_weight[0]
    taps = dw_kernel[0].reshape(TAPS, GROUPS, LANES)
    saved_pair = pair_view(saved[:, 0, 0, 0])
    image_pair = pair_view(images[:, 0, 0])
    head_pair = pair_view(head_grads[:, 0, 0])

    grad_in0, g0, w, t, pair, x0 = call(
        backward_first,
        [HBM] * 5,
        (MESSAGE, MESSAGE)
        + tuple(
            jax.ShapeDtypeStruct(shape, kind)
            for shape, kind in (
                ((C, C), bf16),
                ((TAPS, GROUPS, LANES), f32),
                (PAIR.shape, bf16),
                (TILED.shape, bf16),
            )
        ),
        [TILED, ROWS, PADDED, DENSE, DENSE, WIDE, sems(8)],
        (incoming[0, 0, 0], saved_pair, weight, taps, activations[0, 0, 0]),
    )
    g1 = shifted(grad_in0, -1)
    keep, send = call(
        factors_kernel,
        [VMEM, VMEM, VMEM, ANY],
        (MESSAGE, jax.ShapeDtypeStruct((PIX, 2 * C), bf16)),
        [PADDED, DENSE, WIDE],
        (pair, g0, t, grad_in0),
    )
    peer = other_core(send)
    out0 = call(
        forward_first,
        [VMEM, VMEM, VMEM, ANY],
        MESSAGE,
        [ROWS, PADDED, DENSE, MIXED],
        (x0, w, t, keep),
    )
    act1 = shifted(out0, 1)
    g1 = call(
        head_kernel,
        [ANY, HBM, ANY],
        MESSAGE,
        [PAIR, WIDE, MIXED, sems(1)],
        (g1, head_pair, out0),
        outs=ANY,
        input_output_aliases={0: 0},
    )
    g1_peer = other_core(g1)
    total = call(
        weight_first,
        [VMEM] * 3,
        jax.ShapeDtypeStruct((HALF, C), f32),
        [],
        (keep, g0, peer),
    )
    own, other = call(
        weight_second,
        [VMEM] * 5,
        (jax.ShapeDtypeStruct((QUARTER, C), f32), jax.ShapeDtypeStruct((QUARTER, C), bf16)),
        [],
        (total, keep, g1, peer, g1_peer),
    )
    arrived = other_chip(other)
    grad_in1 = call(
        backward_second,
        [VMEM, VMEM, VMEM, VMEM, ANY],
        LONGER,
        [ROWS, PADDED, DENSE, DENSE, WIDE],
        (g1, pair, w, t, other),
    )
    g2 = shifted(grad_in1, -1)
    small = jax.ShapeDtypeStruct((TAPS, QUARTER), bf16)
    own_k, core_k, chip_k, both_k = call(
        taps_kernel,
        [VMEM] * 4 + [ANY],
        (jax.ShapeDtypeStruct((TAPS, QUARTER), f32), small, small, small),
        [PADDED, PADDED, pltpu.VMEM((32, C), f32), WIDE],
        (pair, g0, g1, w, grad_in1),
    )
    out1 = call(
        forward_second,
        [VMEM] * 3 + [HBM, ANY],
        MESSAGE,
        [ROWS, PADDED, DENSE, MIXED, PAIR, WIDE, sems(1)],
        (act1, w, t, image_pair, own_k),
    )
    act2 = shifted(out1, 1)

    k_grad = call(
        taps_final,
        [VMEM] * 4,
        jax.ShapeDtypeStruct((TAPS, 2, LANES), f32),
        [],
        (own_k, other_core(core_k), other_chip(chip_k), other_both(both_k)),
    )
    w_grad = call(
        final_kernel, [VMEM, VMEM], jax.ShapeDtypeStruct((QUARTER, C), f32), [], (own, arrived)
    )
    grad_out = call(
        functools.partial(unpack_kernel, is_last),
        [ANY, HBM, HBM],
        IMAGE,
        [pltpu.VMEM((PIX_ROWS, C), bf16), ROWS, PAIR, WIDE, sems(1)],
        (g2, head_pair, w_grad),
    )
    act_out = call(
        functools.partial(unpack_kernel, is_first),
        [ANY, HBM, HBM],
        IMAGE,
        [MIXED, ROWS, PAIR, WIDE, sems(1)],
        (act2, image_pair, grad_out),
    )
    k_grad = k_grad.reshape(TAPS, QUARTER)
    return (act_out[None, None, None], grad_out[None, None, None], w_grad[None], k_grad[None])


def solution(mesh):
    in_specs = (
        P("section", "dp", None, None, None, None),
        P("section", "dp", None, None, None, None),
        P(None, "section", "dp", None, None, None, None),
        P(None, "dp", None, None, None, None),
        P(None, "dp", None, None, None, None),
        P("section", None, None),
        P("section", None, None),
    )
    out_specs = (
        P("section", "dp", None, None, None, None),
        P("section", "dp", None, None, None, None),
        P("section", "dp", None),
        P("section", None, "dp"),
    )
    return jax.shard_map(
        per_device, mesh=mesh, in_specs=in_specs, out_specs=out_specs, check_vma=False
    )
```

```python
import functools

import jax
import jax.numpy as jnp
from jax import lax
from jax.experimental import pallas as pl
from jax.experimental.pallas import tpu as pltpu
from jax.sharding import PartitionSpec as P

KW = 5
TAPS = KW * KW
TICKS = 2
HW = 14
PIX = HW * HW
PIX_ROWS = -(-PIX // 8) * 8
C = 1024
LANES = 128
GROUPS = C // LANES
ROW = HW * GROUPS
HALF = C // 2
QUARTER = C // 4
FIRST = 160
SECOND = QUARTER - FIRST
TAP_ROWS = 32
HALF_ROWS = TAP_ROWS // 2
PAD_ROWS = (HW + KW - 1) * ROW
DENSE_ROWS = PIX * GROUPS
TOP = (KW // 2) * ROW

f32 = jnp.float32
bf16 = jnp.bfloat16


def cols(group):
    return slice(group * LANES, (group + 1) * LANES)


def zero_pad(spread):
    zeros = jnp.zeros((TOP, LANES), f32)
    spread[0:TOP, :] = zeros
    spread[PAD_ROWS - TOP : PAD_ROWS, :] = zeros


def tile_at(spread, pixel):
    return spread[pl.ds(pl.multiple_of(pixel * GROUPS, GROUPS), GROUPS), :]


def conv(padded, taps, emit, flip):
    def row(p, carry):
        acc = [None] * HW
        for a in range(KW):
            tiles = [tile_at(padded, (p + a) * HW + q) for q in range(HW)]
            for b in range(KW):
                index = KW * a + b
                tap = taps[TAPS - 1 - index if flip else index]
                for q in range(HW):
                    src = q + b - KW // 2
                    if 0 <= src < HW:
                        term = tiles[src] * tap
                        acc[q] = term if acc[q] is None else acc[q] + term
        for q in range(HW):
            emit(p * HW + q, acc[q])
        return carry

    lax.fori_loop(0, HW, row, 0)


def tap_sums(rect_padded, grad_padded):
    def row(p, acc):
        acc = list(acc)
        grads = [tile_at(grad_padded, (p + KW // 2) * HW + q) for q in range(HW)]
        for a in range(KW):
            tiles = [tile_at(rect_padded, (p + a) * HW + q) for q in range(HW)]
            for b in range(KW):
                index = KW * a + b
                for q in range(HW):
                    src = q + b - KW // 2
                    if 0 <= src < HW:
                        acc[index] = acc[index] + tiles[src] * grads[q]
        return tuple(acc)

    return lax.fori_loop(0, HW, row, (jnp.zeros((GROUPS, LANES), f32),) * TAPS)


def store_tile(dense):
    def emit(pixel, value):
        dense[pl.ds(pl.multiple_of(pixel * GROUPS, GROUPS), GROUPS), :] = value

    return emit


def spread_rows(padded, group, value):
    padded[pl.ds(TOP + group, PIX, stride=GROUPS), :] = value


def rows_of(dense, group):
    return dense[pl.ds(group, PIX, stride=GROUPS), :]


def pack_rows(image, dst):
    for p in range(HW):
        dst[p * HW : (p + 1) * HW, :] = image[p].astype(f32)


def widen_pair(pair, wide):
    def step(p, carry):
        wide[pl.ds(pl.multiple_of(p * HW * 16, 16), HW * 16), :] = (
            pair[pl.ds(p * HW, HW)].astype(f32).reshape(HW * 16, LANES)
        )
        return carry

    lax.fori_loop(0, HW, step, 0)


def pair_tick_spread(wide, tick):
    return wide[pl.ds(tick, DENSE_ROWS, stride=TICKS), :]


def pair_tick_rows(wide, tick, group):
    return wide[pl.ds(tick + TICKS * group, PIX, stride=TICKS * GROUPS), :]


def replace_at_edge(edge, pair_hbm, tick, pair, wide, rows, sem):
    @pl.when(edge)
    def _():
        fetch(pair_hbm, pair, sem)
        widen_pair(pair, wide)
        for group in range(GROUPS):
            rows[:, cols(group)] = pair_tick_rows(wide, tick, group).astype(rows.dtype)


def fetch(src, dst, sem):
    copy = pltpu.make_async_copy(src, dst, sem)
    copy.start()
    copy.wait()


def is_first():
    return lax.axis_index("section") == 0


def is_last():
    return lax.axis_index("section") == lax.axis_size("section") - 1


def mix(rows, padded, dense, mixed, taps):
    zero_pad(padded)
    for group in range(GROUPS):
        spread_rows(padded, group, jnp.maximum(rows[:, cols(group)], 0.0))
    conv(padded, taps, store_tile(dense), False)
    for group in range(GROUPS):
        mixed[:, cols(group)] = rows_of(dense, group).astype(bf16)


def forward_first(x, weight, taps, token, out, rows, padded, dense, mixed):
    pack_rows(x, rows)
    mix(rows, padded, dense, mixed, taps)
    out[...] = (rows[...] + jnp.dot(mixed[...], weight[...], preferred_element_type=f32)).astype(bf16)


def forward_second(x, weight, taps, images, token, out, rows, padded, dense, mixed, pair, wide, sem):
    rows[...] = x[...].astype(f32)
    replace_at_edge(is_first(), images, 0, pair, wide, rows, sem)
    mix(rows, padded, dense, mixed, taps)
    out[...] = (rows[...] + jnp.dot(mixed[...], weight[...], preferred_element_type=f32)).astype(bf16)


def head_kernel(g_in, heads, token, g_out, pair, wide, rows, sem):
    @pl.when(is_last())
    def _():
        fetch(heads, pair, sem)
        widen_pair(pair, wide)
        for group in range(GROUPS):
            rows[:, cols(group)] = pair_tick_rows(wide, 0, group).astype(bf16)
        fetch(rows, g_out, sem)


def spread_grad(g, weight, grad_mixed, waits=()):
    zero_pad(grad_mixed)
    for block in range(4):
        if waits:
            waits[block].wait()
        product = lax.dot_general(
            g[...],
            weight[block * QUARTER : (block + 1) * QUARTER, :],
            (((1,), (1,)), ((), ())),
            preferred_element_type=f32,
        )
        for part in range(2):
            spread_rows(grad_mixed, 2 * block + part, product[:, cols(part)])


def finish_backward(taps, out, grad_mixed, rows, dense, mask):
    def emit(pixel, value):
        keep = tile_at(mask, pixel) > 0.0
        store_tile(dense)(pixel, jnp.where(keep, value, 0.0))

    conv(grad_mixed, taps, emit, True)
    for group in range(GROUPS):
        out[0:PIX, cols(group)] = (rows[:, cols(group)] + rows_of(dense, group)).astype(bf16)


def backward_first(
    g_hbm, saved, w_hbm, taps_hbm, x_hbm, out, g_rows, weight, taps, pair, x, g, rows, grad_mixed, dense, mask, wide, sems
):
    blocks = [slice(block * QUARTER, (block + 1) * QUARTER) for block in range(4)]
    pieces = [(g_hbm, g), (saved, pair)]
    pieces += [(w_hbm.at[rows_, :], weight.at[rows_, :]) for rows_ in blocks]
    pieces += [(taps_hbm, taps), (x_hbm, x)]
    copies = [
        pltpu.make_async_copy(src, dst, sems.at[i]) for i, (src, dst) in enumerate(pieces)
    ]
    for copy in copies:
        copy.start()
    copies[0].wait()
    pack_rows(g, rows)
    g_rows[...] = rows[...].astype(bf16)
    copies[1].wait()
    widen_pair(pair, wide)
    mask[...] = pair_tick_spread(wide, 0)
    spread_grad(g_rows, weight, grad_mixed, copies[2:6])
    copies[6].wait()
    finish_backward(taps, out, grad_mixed, rows, dense, mask)
    copies[7].wait()


def backward_second(g, pair, weight, taps, token, out, rows, grad_mixed, dense, mask, wide):
    widen_pair(pair, wide)
    mask[...] = pair_tick_spread(wide, 1)
    rows[...] = g[...].astype(f32)
    spread_grad(g, weight, grad_mixed)
    out[PIX:PIX_ROWS, :] = jnp.zeros((PIX_ROWS - PIX, C), bf16)
    finish_backward(taps, out, grad_mixed, rows, dense, mask)


def factors_kernel(pair, g_rows, taps, token, keep, send, padded, dense, wide):
    core = lax.rem(lax.axis_index("dp"), 2)
    high = lax.div(lax.axis_index("dp"), 2)
    widen_pair(pair, wide)
    send[:, C : 2 * C] = g_rows[...]
    zero_pad(padded)
    for tick in range(TICKS):
        padded[TOP : TOP + DENSE_ROWS, :] = jnp.maximum(pair_tick_spread(wide, tick), 0.0)
        conv(padded, taps, store_tile(dense), False)
        for place in range(2):
            side = high if place == 0 else 1 - high
            for part in range(2):
                at = tick * HALF + (2 * place + part) * LANES
                mine = 4 * side + 2 * core + part
                theirs = 4 * side + 2 * (1 - core) + part
                keep[:, at : at + LANES] = rows_of(dense, mine).astype(bf16)
                send[:, at : at + LANES] = rows_of(dense, theirs).astype(bf16)


def weight_term(factor, grads):
    return lax.dot_general(factor, grads, (((0,), (0,)), ((), ())), preferred_element_type=f32)


def weight_first(keep, g_own, peer, out):
    out[...] = weight_term(keep[:, :HALF], g_own[...])
    out[...] += weight_term(peer[:, :HALF], peer[:, C : 2 * C])


def weight_second(total, keep, g_own, peer, g_peer, token, own, other_top, other_low):
    for place in range(2):
        rows = slice(place * QUARTER, (place + 1) * QUARTER)
        part = slice(HALF + place * QUARTER, HALF + (place + 1) * QUARTER)
        value = total[rows, :] + weight_term(keep[:, part], g_own[...])
        value += weight_term(peer[:, part], g_peer[...])
        if place == 0:
            own[...] = value
        else:
            other_top[...] = value[0:FIRST, :].astype(bf16)
            other_low[...] = value[FIRST:QUARTER, :].astype(bf16)


def taps_kernel(pair, g0, g1, weight, token, mine, theirs, rect, grad, sums, wide):
    core = lax.rem(lax.axis_index("dp"), 2)
    high = lax.div(lax.axis_index("dp"), 2)
    widen_pair(pair, wide)
    zero_pad(rect)
    for tick in range(TICKS):
        rect[TOP : TOP + DENSE_ROWS, :] = jnp.maximum(pair_tick_spread(wide, tick), 0.0)
        spread_grad((g0, g1)[tick], weight, grad)
        terms = tap_sums(rect, grad)
        if tick == 0:
            sums[TAPS:TAP_ROWS, :] = jnp.zeros((TAP_ROWS - TAPS, C), f32)
        for index in range(TAPS):
            row = jnp.concatenate([terms[index][i : i + 1] for i in range(GROUPS)], axis=1)
            if tick == 0:
                sums[index : index + 1, :] = row
            else:
                sums[index : index + 1, :] += row

    def block(side, which):
        at = pl.multiple_of((2 * side + which) * QUARTER, QUARTER)
        return sums[:, pl.ds(at, QUARTER)]

    for place in range(2):
        side = high if place == 0 else 1 - high
        at = slice(place * QUARTER, (place + 1) * QUARTER)
        mine[:, at] = block(side, core)
        theirs[:, at] = block(side, 1 - core).astype(bf16)


def pack_kernel(mine, arrived, other_low, own, message):
    total = mine[...] + arrived[...].astype(f32)
    own[...] = total[:, 0:QUARTER]
    message[0:SECOND, :] = other_low[...]
    for part in range(2):
        taps = total[part * HALF_ROWS : (part + 1) * HALF_ROWS, QUARTER:HALF]
        message[SECOND:, part * QUARTER : (part + 1) * QUARTER] = taps.astype(bf16)
    message[SECOND:, HALF:] = jnp.zeros((HALF_ROWS, HALF), bf16)


SCALE = 1.0 / (2 * 2 * TICKS)


def final_kernel(own, top, low, own_k, out, out_k, taps):
    out[0:FIRST, :] = (own[0:FIRST, :] + top[...].astype(f32)) * SCALE
    out[FIRST:QUARTER, :] = (own[FIRST:QUARTER, :] + low[0:SECOND, :].astype(f32)) * SCALE
    for part in range(2):
        rows = slice(part * HALF_ROWS, (part + 1) * HALF_ROWS)
        arrived = low[SECOND:, part * QUARTER : (part + 1) * QUARTER].astype(f32)
        taps[rows, :] = (own_k[rows, :] + arrived) * SCALE
    for part in range(2):
        out_k[:, part, :] = taps[0:TAPS, cols(part)]


def unpack_kernel(edge, message, images, token, out, packed, rows, pair, wide, sem):
    fetch(message, packed, sem)
    rows[...] = packed[0:PIX, :].astype(f32)
    replace_at_edge(edge(), images, 1, pair, wide, rows, sem)
    for p in range(HW):
        out[p] = rows[p * HW : (p + 1) * HW, :].astype(bf16)


VMEM = pl.BlockSpec(memory_space=pltpu.VMEM)
HBM = pl.BlockSpec(memory_space=pltpu.HBM)
ANY = pl.BlockSpec(memory_space=pl.ANY)


def call(kernel, ins, out_shape, scratch, args, cost=1, outs=None, **options):
    pinned = [in_hbm(arg) if spec is HBM else arg for spec, arg in zip(ins, args)]
    return pl.pallas_call(
        kernel,
        in_specs=ins,
        out_specs=jax.tree.map(lambda _: VMEM, out_shape) if outs is None else outs,
        out_shape=out_shape,
        scratch_shapes=scratch,
        compiler_params=pltpu.CompilerParams(vmem_limit_bytes=20 * 1024 * 1024),
        cost_estimate=pl.CostEstimate(flops=0, bytes_accessed=cost << 10, transcendentals=0),
        **options,
    )(*pinned)


def in_hbm(array):
    return pltpu.with_memory_space_constraint(array, pltpu.HBM)


PAIR = pltpu.VMEM((PIX, TICKS * GROUPS, LANES), bf16)
WIDE = pltpu.VMEM((PIX * TICKS * GROUPS, LANES), f32)
ROWS = pltpu.VMEM((PIX, C), f32)
PADDED = pltpu.VMEM((PAD_ROWS, LANES), f32)
DENSE = pltpu.VMEM((DENSE_ROWS, LANES), f32)
MIXED = pltpu.VMEM((PIX, C), bf16)
TILED = pltpu.VMEM((HW, HW, C), bf16)
IMAGE = jax.ShapeDtypeStruct((HW, HW, C), bf16)
MESSAGE = jax.ShapeDtypeStruct((PIX, C), bf16)
LONGER = jax.ShapeDtypeStruct((PIX_ROWS, C), bf16)


def sems(count):
    return pltpu.SemaphoreType.DMA((count,)) if count > 1 else pltpu.SemaphoreType.DMA


def pair_view(array):
    moved = jnp.transpose(array, (1, 2, 0, 3)).reshape(HW, HW, TICKS, GROUPS, LANES)
    return jnp.transpose(moved, (0, 1, 3, 2, 4)).reshape(PIX, TICKS * GROUPS, LANES)


def shifted(value, by):
    peers = lax.axis_size("section")
    pairs = [(i, i + by) for i in range(peers) if 0 <= i + by < peers]
    return lax.ppermute(value, "section", pairs)


def other_core(value):
    return lax.ppermute(value, "dp", [(0, 1), (1, 0), (2, 3), (3, 2)])


def other_chip(value):
    return lax.ppermute(value, "dp", [(0, 2), (2, 0), (1, 3), (3, 1)])


def per_device(activations, incoming, saved, images, head_grads, pw_weight, dw_kernel):
    weight = pw_weight[0]
    taps = dw_kernel[0].reshape(TAPS, GROUPS, LANES)
    saved_pair = pair_view(saved[:, 0, 0, 0])
    image_pair = pair_view(images[:, 0, 0])
    head_pair = pair_view(head_grads[:, 0, 0])

    grad_in0, g0, w, t, pair, x0 = call(
        backward_first,
        [HBM] * 5,
        (MESSAGE, MESSAGE)
        + tuple(
            jax.ShapeDtypeStruct(shape, kind)
            for shape, kind in (
                ((C, C), bf16),
                ((TAPS, GROUPS, LANES), f32),
                (PAIR.shape, bf16),
                (TILED.shape, bf16),
            )
        ),
        [TILED, ROWS, PADDED, DENSE, DENSE, WIDE, sems(8)],
        (incoming[0, 0, 0], saved_pair, weight, taps, activations[0, 0, 0]),
    )
    g1 = shifted(grad_in0, -1)
    keep, send = call(
        factors_kernel,
        [VMEM, VMEM, VMEM, ANY],
        (MESSAGE, jax.ShapeDtypeStruct((PIX, 2 * C), bf16)),
        [PADDED, DENSE, WIDE],
        (pair, g0, t, grad_in0),
    )
    peer = other_core(send)
    out0 = call(
        forward_first,
        [VMEM, VMEM, VMEM, ANY],
        MESSAGE,
        [ROWS, PADDED, DENSE, MIXED],
        (x0, w, t, keep),
    )
    act1 = shifted(out0, 1)
    g1 = call(
        head_kernel,
        [ANY, HBM, ANY],
        MESSAGE,
        [PAIR, WIDE, MIXED, sems(1)],
        (g1, head_pair, out0),
        outs=ANY,
        input_output_aliases={0: 0},
    )
    g1_peer = other_core(g1)
    grad_in1 = call(
        backward_second,
        [VMEM, VMEM, VMEM, VMEM, ANY],
        LONGER,
        [ROWS, PADDED, DENSE, DENSE, WIDE],
        (g1, pair, w, t, out0),
    )
    g2 = shifted(grad_in1, -1)
    out1 = call(
        forward_second,
        [VMEM] * 3 + [HBM, ANY],
        MESSAGE,
        [ROWS, PADDED, DENSE, MIXED, PAIR, WIDE, sems(1)],
        (act1, w, t, image_pair, grad_in1),
    )
    act2 = shifted(out1, 1)

    total = call(
        weight_first,
        [VMEM] * 3,
        jax.ShapeDtypeStruct((HALF, C), f32),
        [],
        (keep, g0, peer),
    )
    own, other_top, other_low = call(
        weight_second,
        [VMEM] * 5 + [ANY],
        (
            jax.ShapeDtypeStruct((QUARTER, C), f32),
            jax.ShapeDtypeStruct((FIRST, C), bf16),
            jax.ShapeDtypeStruct((SECOND, C), bf16),
        ),
        [],
        (total, keep, g1, peer, g1_peer, out1),
    )
    top = other_chip(other_top)
    mine, theirs = call(
        taps_kernel,
        [VMEM] * 4 + [ANY],
        (
            jax.ShapeDtypeStruct((TAP_ROWS, HALF), f32),
            jax.ShapeDtypeStruct((TAP_ROWS, HALF), bf16),
        ),
        [PADDED, PADDED, pltpu.VMEM((TAP_ROWS, C), f32), WIDE],
        (pair, g0, g1, w, other_top),
    )
    own_k, message = call(
        pack_kernel,
        [VMEM] * 3,
        (
            jax.ShapeDtypeStruct((TAP_ROWS, QUARTER), f32),
            jax.ShapeDtypeStruct((SECOND + HALF_ROWS, C), bf16),
        ),
        [],
        (mine, other_core(theirs), other_low),
    )
    low = other_chip(message)
    grad_out = call(
        functools.partial(unpack_kernel, is_last),
        [ANY, HBM, ANY],
        IMAGE,
        [pltpu.VMEM((PIX_ROWS, C), bf16), ROWS, PAIR, WIDE, sems(1)],
        (g2, head_pair, own),
    )
    act_out = call(
        functools.partial(unpack_kernel, is_first),
        [ANY, HBM, ANY],
        IMAGE,
        [MIXED, ROWS, PAIR, WIDE, sems(1)],
        (act2, image_pair, own),
    )
    w_grad, k_grad = call(
        final_kernel,
        [VMEM] * 4,
        (
            jax.ShapeDtypeStruct((QUARTER, C), f32),
            jax.ShapeDtypeStruct((TAPS, 2, LANES), f32),
        ),
        [pltpu.VMEM((TAP_ROWS, QUARTER), f32)],
        (own, top, low, own_k),
    )
    k_grad = k_grad.reshape(TAPS, QUARTER)
    return (act_out[None, None, None], grad_out[None, None, None], w_grad[None], k_grad[None])


def solution(mesh):
    in_specs = (
        P("section", "dp", None, None, None, None),
        P("section", "dp", None, None, None, None),
        P(None, "section", "dp", None, None, None, None),
        P(None, "dp", None, None, None, None),
        P(None, "dp", None, None, None, None),
        P("section", None, None),
        P("section", None, None),
    )
    out_specs = (
        P("section", "dp", None, None, None, None),
        P("section", "dp", None, None, None, None),
        P("section", "dp", None),
        P("section", None, "dp"),
    )
    return jax.shard_map(
        per_device, mesh=mesh, in_specs=in_specs, out_specs=out_specs, check_vma=False
    )
```

```python
import functools

import jax
import jax.numpy as jnp
from jax import lax
from jax.experimental import pallas as pl
from jax.experimental.pallas import tpu as pltpu
from jax.sharding import PartitionSpec as P

KW = 5
TAPS = KW * KW
TICKS = 2
HW = 14
PIX = HW * HW
PIX_ROWS = -(-PIX // 8) * 8
ACT_ROWS = 216
C = 1024
LANES = 128
GROUPS = C // LANES
ROW = HW * GROUPS
HALF = C // 2
QUARTER = C // 4
FIRST = 208
SECOND = QUARTER - FIRST
TAP_ROWS = 32
LAST_ROWS = TAP_ROWS // 4
PAD_ROWS = (HW + KW - 1) * ROW
DENSE_ROWS = PIX * GROUPS
TOP = (KW // 2) * ROW

f32 = jnp.float32
bf16 = jnp.bfloat16


def cols(group):
    return slice(group * LANES, (group + 1) * LANES)


def zero_pad(spread):
    zeros = jnp.zeros((TOP, LANES), f32)
    spread[0:TOP, :] = zeros
    spread[PAD_ROWS - TOP : PAD_ROWS, :] = zeros


def tile_at(spread, pixel):
    return spread[pl.ds(pl.multiple_of(pixel * GROUPS, GROUPS), GROUPS), :]


def conv(padded, taps, emit, flip):
    def row(p, carry):
        acc = [None] * HW
        for a in range(KW):
            tiles = [tile_at(padded, (p + a) * HW + q) for q in range(HW)]
            for b in range(KW):
                index = KW * a + b
                tap = taps[TAPS - 1 - index if flip else index]
                for q in range(HW):
                    src = q + b - KW // 2
                    if 0 <= src < HW:
                        term = tiles[src] * tap
                        acc[q] = term if acc[q] is None else acc[q] + term
        for q in range(HW):
            emit(p * HW + q, acc[q])
        return carry

    lax.fori_loop(0, HW, row, 0)


def tap_sums(rect_padded, grad_padded):
    def row(p, acc):
        acc = list(acc)
        grads = [tile_at(grad_padded, (p + KW // 2) * HW + q) for q in range(HW)]
        for a in range(KW):
            tiles = [tile_at(rect_padded, (p + a) * HW + q) for q in range(HW)]
            for b in range(KW):
                index = KW * a + b
                for q in range(HW):
                    src = q + b - KW // 2
                    if 0 <= src < HW:
                        acc[index] = acc[index] + tiles[src] * grads[q]
        return tuple(acc)

    return lax.fori_loop(0, HW, row, (jnp.zeros((GROUPS, LANES), f32),) * TAPS)


def store_tile(dense):
    def emit(pixel, value):
        dense[pl.ds(pl.multiple_of(pixel * GROUPS, GROUPS), GROUPS), :] = value

    return emit


def spread_rows(padded, group, value):
    padded[pl.ds(TOP + group, PIX, stride=GROUPS), :] = value


def rows_of(dense, group):
    return dense[pl.ds(group, PIX, stride=GROUPS), :]


def pack_rows(image, dst):
    for p in range(HW):
        dst[p * HW : (p + 1) * HW, :] = image[p].astype(f32)


def widen_pair(pair, wide):
    def step(p, carry):
        wide[pl.ds(pl.multiple_of(p * HW * 16, 16), HW * 16), :] = (
            pair[pl.ds(p * HW, HW)].astype(f32).reshape(HW * 16, LANES)
        )
        return carry

    lax.fori_loop(0, HW, step, 0)


def pair_tick_spread(wide, tick):
    return wide[pl.ds(tick, DENSE_ROWS, stride=TICKS), :]


def pair_tick_rows(wide, tick, group):
    return wide[pl.ds(tick + TICKS * group, PIX, stride=TICKS * GROUPS), :]


def replace_at_edge(edge, pair_hbm, tick, pair, wide, rows, sem):
    @pl.when(edge)
    def _():
        fetch(pair_hbm, pair, sem)
        widen_pair(pair, wide)
        for group in range(GROUPS):
            rows[:, cols(group)] = pair_tick_rows(wide, tick, group).astype(rows.dtype)


def fetch(src, dst, sem):
    copy = pltpu.make_async_copy(src, dst, sem)
    copy.start()
    copy.wait()


def is_first():
    return lax.axis_index("section") == 0


def is_last():
    return lax.axis_index("section") == lax.axis_size("section") - 1


def mix(rows, padded, dense, mixed, taps):
    zero_pad(padded)
    for group in range(GROUPS):
        spread_rows(padded, group, jnp.maximum(rows[:, cols(group)], 0.0))
    conv(padded, taps, store_tile(dense), False)
    for group in range(GROUPS):
        mixed[:, cols(group)] = rows_of(dense, group).astype(bf16)


def forward_first(x, weight, taps, token, out, rows, padded, dense, mixed):
    pack_rows(x, rows)
    mix(rows, padded, dense, mixed, taps)
    out[PIX:ACT_ROWS, :] = jnp.zeros((ACT_ROWS - PIX, C), bf16)
    out[0:PIX, :] = (rows[...] + jnp.dot(mixed[...], weight[...], preferred_element_type=f32)).astype(bf16)


def forward_second(x, weight, taps, images, token, out, rows, padded, dense, mixed, pair, wide, sem):
    rows[...] = x[0:PIX, :].astype(f32)
    replace_at_edge(is_first(), images, 0, pair, wide, rows, sem)
    mix(rows, padded, dense, mixed, taps)
    out[...] = (rows[...] + jnp.dot(mixed[...], weight[...], preferred_element_type=f32)).astype(bf16)


def head_kernel(g_in, heads, token, g_out, pair, wide, rows, sem):
    @pl.when(is_last())
    def _():
        fetch(heads, pair, sem)
        widen_pair(pair, wide)
        for group in range(GROUPS):
            rows[:, cols(group)] = pair_tick_rows(wide, 0, group).astype(bf16)
        fetch(rows, g_out, sem)


def spread_grad(g, weight, grad_mixed, waits=()):
    zero_pad(grad_mixed)
    for block in range(4):
        if waits:
            waits[block].wait()
        product = lax.dot_general(
            g[...],
            weight[block * QUARTER : (block + 1) * QUARTER, :],
            (((1,), (1,)), ((), ())),
            preferred_element_type=f32,
        )
        for part in range(2):
            spread_rows(grad_mixed, 2 * block + part, product[:, cols(part)])


def finish_backward(taps, out, grad_mixed, rows, dense, mask):
    def emit(pixel, value):
        keep = tile_at(mask, pixel) > 0.0
        store_tile(dense)(pixel, jnp.where(keep, value, 0.0))

    conv(grad_mixed, taps, emit, True)
    for group in range(GROUPS):
        out[0:PIX, cols(group)] = (rows[:, cols(group)] + rows_of(dense, group)).astype(bf16)


def backward_first(
    g_hbm, saved, w_hbm, taps_hbm, x_hbm, out, g_rows, weight, taps, pair, x, g, rows, grad_mixed, dense, mask, wide, sems
):
    blocks = [slice(block * QUARTER, (block + 1) * QUARTER) for block in range(4)]
    pieces = [(g_hbm, g)]
    pieces += [(w_hbm.at[rows_, :], weight.at[rows_, :]) for rows_ in blocks]
    pieces += [(saved, pair), (taps_hbm, taps), (x_hbm, x)]
    copies = [
        pltpu.make_async_copy(src, dst, sems.at[i]) for i, (src, dst) in enumerate(pieces)
    ]
    for copy in copies:
        copy.start()
    copies[0].wait()
    pack_rows(g, rows)
    g_rows[...] = rows[...].astype(bf16)
    spread_grad(g_rows, weight, grad_mixed, copies[1:5])
    copies[5].wait()
    widen_pair(pair, wide)
    mask[...] = pair_tick_spread(wide, 0)
    copies[6].wait()
    finish_backward(taps, out, grad_mixed, rows, dense, mask)
    copies[7].wait()


def backward_second(g, pair, weight, taps, token, out, rows, grad_mixed, dense, mask, wide):
    widen_pair(pair, wide)
    mask[...] = pair_tick_spread(wide, 1)
    rows[...] = g[...].astype(f32)
    spread_grad(g, weight, grad_mixed)
    out[PIX:PIX_ROWS, :] = jnp.zeros((PIX_ROWS - PIX, C), bf16)
    finish_backward(taps, out, grad_mixed, rows, dense, mask)


def factors_kernel(pair, g_rows, taps, token, keep, send, padded, dense, wide):
    core = lax.rem(lax.axis_index("dp"), 2)
    high = lax.div(lax.axis_index("dp"), 2)
    widen_pair(pair, wide)
    send[:, C : 2 * C] = g_rows[...]
    zero_pad(padded)
    for tick in range(TICKS):
        padded[TOP : TOP + DENSE_ROWS, :] = jnp.maximum(pair_tick_spread(wide, tick), 0.0)
        conv(padded, taps, store_tile(dense), False)
        for place in range(2):
            side = high if place == 0 else 1 - high
            for part in range(2):
                at = tick * HALF + (2 * place + part) * LANES
                mine = 4 * side + 2 * core + part
                theirs = 4 * side + 2 * (1 - core) + part
                keep[:, at : at + LANES] = rows_of(dense, mine).astype(bf16)
                send[:, at : at + LANES] = rows_of(dense, theirs).astype(bf16)


def weight_term(factor, grads):
    return lax.dot_general(factor, grads, (((0,), (0,)), ((), ())), preferred_element_type=f32)


def weight_first(keep, g_own, peer, out):
    out[...] = weight_term(keep[:, :HALF], g_own[...])
    out[...] += weight_term(peer[:, :HALF], peer[:, C : 2 * C])


def weight_second(total, keep, g_own, peer, g_peer, token, own_top, own_low, other_top, other_low):
    for place in range(2):
        rows = slice(place * QUARTER, (place + 1) * QUARTER)
        part = slice(HALF + place * QUARTER, HALF + (place + 1) * QUARTER)
        value = total[rows, :] + weight_term(keep[:, part], g_own[...])
        value += weight_term(peer[:, part], g_peer[...])
        if place == 0:
            own_top[...] = value[0:FIRST, :]
            own_low[...] = value[FIRST:QUARTER, :]
        else:
            other_top[...] = value[0:FIRST, :].astype(bf16)
            other_low[...] = value[FIRST:QUARTER, :].astype(bf16)


def taps_kernel(pair, g0, g1, weight, token, mine, theirs, rect, grad, sums, wide):
    core = lax.rem(lax.axis_index("dp"), 2)
    high = lax.div(lax.axis_index("dp"), 2)
    widen_pair(pair, wide)
    zero_pad(rect)
    for tick in range(TICKS):
        rect[TOP : TOP + DENSE_ROWS, :] = jnp.maximum(pair_tick_spread(wide, tick), 0.0)
        spread_grad((g0, g1)[tick], weight, grad)
        terms = tap_sums(rect, grad)
        if tick == 0:
            sums[TAPS:TAP_ROWS, :] = jnp.zeros((TAP_ROWS - TAPS, C), f32)
        for index in range(TAPS):
            row = jnp.concatenate([terms[index][i : i + 1] for i in range(GROUPS)], axis=1)
            if tick == 0:
                sums[index : index + 1, :] = row
            else:
                sums[index : index + 1, :] += row

    def block(side, which):
        at = pl.multiple_of((2 * side + which) * QUARTER, QUARTER)
        return sums[:, pl.ds(at, QUARTER)]

    for place in range(2):
        side = high if place == 0 else 1 - high
        at = slice(place * QUARTER, (place + 1) * QUARTER)
        mine[:, at] = block(side, core)
        theirs[:, at] = block(side, 1 - core).astype(bf16)


def pack_kernel(mine, arrived, other_low, own, message):
    total = mine[...] + arrived[...].astype(f32)
    own[...] = total[:, 0:QUARTER]
    message[0:SECOND, :] = other_low[...]
    for part in range(4):
        taps = total[part * LAST_ROWS : (part + 1) * LAST_ROWS, QUARTER:HALF]
        message[SECOND:, part * QUARTER : (part + 1) * QUARTER] = taps.astype(bf16)


SCALE = 1.0 / (2 * 2 * TICKS)


def final_first(own, top, out, rows, sem):
    rows[...] = (own[...] + top[...].astype(f32)) * SCALE
    fetch(rows, out.at[0:FIRST, :], sem)


def final_second(own, low, own_k, grads, out, out_k, rows, taps, sem):
    rows[...] = (own[...] + low[0:SECOND, :].astype(f32)) * SCALE
    copy = pltpu.make_async_copy(rows, out.at[FIRST:QUARTER, :], sem)
    copy.start()
    for part in range(4):
        at = slice(part * LAST_ROWS, (part + 1) * LAST_ROWS)
        arrived = low[SECOND:, part * QUARTER : (part + 1) * QUARTER].astype(f32)
        taps[at, :] = (own_k[at, :] + arrived) * SCALE
    for part in range(2):
        out_k[:, part, :] = taps[0:TAPS, cols(part)]
    copy.wait()


def unpack_kernel(edge, message, images, token, out, packed, rows, pair, wide, sem):
    fetch(message, packed, sem)
    rows[...] = packed[0:PIX, :].astype(f32)
    replace_at_edge(edge(), images, 1, pair, wide, rows, sem)
    for p in range(HW):
        out[p] = rows[p * HW : (p + 1) * HW, :].astype(bf16)


VMEM = pl.BlockSpec(memory_space=pltpu.VMEM)
HBM = pl.BlockSpec(memory_space=pltpu.HBM)
ANY = pl.BlockSpec(memory_space=pl.ANY)


def call(kernel, ins, out_shape, scratch, args, cost=1, outs=None, **options):
    pinned = [in_hbm(arg) if spec is HBM else arg for spec, arg in zip(ins, args)]
    return pl.pallas_call(
        kernel,
        in_specs=ins,
        out_specs=jax.tree.map(lambda _: VMEM, out_shape) if outs is None else outs,
        out_shape=out_shape,
        scratch_shapes=scratch,
        compiler_params=pltpu.CompilerParams(vmem_limit_bytes=20 * 1024 * 1024),
        cost_estimate=pl.CostEstimate(flops=0, bytes_accessed=cost << 10, transcendentals=0),
        **options,
    )(*pinned)


def in_hbm(array):
    return pltpu.with_memory_space_constraint(array, pltpu.HBM)


PAIR = pltpu.VMEM((PIX, TICKS * GROUPS, LANES), bf16)
WIDE = pltpu.VMEM((PIX * TICKS * GROUPS, LANES), f32)
ROWS = pltpu.VMEM((PIX, C), f32)
PADDED = pltpu.VMEM((PAD_ROWS, LANES), f32)
DENSE = pltpu.VMEM((DENSE_ROWS, LANES), f32)
MIXED = pltpu.VMEM((PIX, C), bf16)
TILED = pltpu.VMEM((HW, HW, C), bf16)
IMAGE = jax.ShapeDtypeStruct((HW, HW, C), bf16)
MESSAGE = jax.ShapeDtypeStruct((PIX, C), bf16)
LONGER = jax.ShapeDtypeStruct((PIX_ROWS, C), bf16)
ACTS = jax.ShapeDtypeStruct((ACT_ROWS, C), bf16)


def sems(count):
    return pltpu.SemaphoreType.DMA((count,)) if count > 1 else pltpu.SemaphoreType.DMA


def pair_view(array):
    moved = jnp.transpose(array, (1, 2, 0, 3)).reshape(HW, HW, TICKS, GROUPS, LANES)
    return jnp.transpose(moved, (0, 1, 3, 2, 4)).reshape(PIX, TICKS * GROUPS, LANES)


def shifted(value, by):
    peers = lax.axis_size("section")
    pairs = [(i, i + by) for i in range(peers) if 0 <= i + by < peers]
    return lax.ppermute(value, "section", pairs)


def other_core(value):
    return lax.ppermute(value, "dp", [(0, 1), (1, 0), (2, 3), (3, 2)])


def other_chip(value):
    return lax.ppermute(value, "dp", [(0, 2), (2, 0), (1, 3), (3, 1)])


def per_device(activations, incoming, saved, images, head_grads, pw_weight, dw_kernel):
    weight = pw_weight[0]
    taps = dw_kernel[0].reshape(TAPS, GROUPS, LANES)
    saved_pair = pair_view(saved[:, 0, 0, 0])
    image_pair = pair_view(images[:, 0, 0])
    head_pair = pair_view(head_grads[:, 0, 0])

    grad_in0, g0, w, t, pair, x0 = call(
        backward_first,
        [HBM] * 5,
        (MESSAGE, MESSAGE)
        + tuple(
            jax.ShapeDtypeStruct(shape, kind)
            for shape, kind in (
                ((C, C), bf16),
                ((TAPS, GROUPS, LANES), f32),
                (PAIR.shape, bf16),
                (TILED.shape, bf16),
            )
        ),
        [TILED, ROWS, PADDED, DENSE, DENSE, WIDE, sems(8)],
        (incoming[0, 0, 0], saved_pair, weight, taps, activations[0, 0, 0]),
    )
    g1 = shifted(grad_in0, -1)
    keep, send = call(
        factors_kernel,
        [VMEM, VMEM, VMEM, ANY],
        (MESSAGE, jax.ShapeDtypeStruct((PIX, 2 * C), bf16)),
        [PADDED, DENSE, WIDE],
        (pair, g0, t, grad_in0),
    )
    peer = other_core(send)
    out0 = call(
        forward_first,
        [VMEM, VMEM, VMEM, ANY],
        ACTS,
        [ROWS, PADDED, DENSE, MIXED],
        (x0, w, t, keep),
    )
    act1 = shifted(out0, 1)
    g1 = call(
        head_kernel,
        [ANY, HBM, ANY],
        MESSAGE,
        [PAIR, WIDE, MIXED, sems(1)],
        (g1, head_pair, out0),
        outs=ANY,
        input_output_aliases={0: 0},
    )
    g1_peer = other_core(g1)

    total = call(
        weight_first,
        [VMEM] * 3,
        jax.ShapeDtypeStruct((HALF, C), f32),
        [],
        (keep, g0, peer),
    )
    own_top, own_low, other_top, other_low = call(
        weight_second,
        [VMEM] * 5 + [ANY],
        (
            jax.ShapeDtypeStruct((FIRST, C), f32),
            jax.ShapeDtypeStruct((SECOND, C), f32),
            jax.ShapeDtypeStruct((FIRST, C), bf16),
            jax.ShapeDtypeStruct((SECOND, C), bf16),
        ),
        [],
        (total, keep, g1, peer, g1_peer, out0),
    )
    top = other_chip(other_top)
    grad_in1 = call(
        backward_second,
        [VMEM, VMEM, VMEM, VMEM, ANY],
        LONGER,
        [ROWS, PADDED, DENSE, DENSE, WIDE],
        (g1, pair, w, t, other_top),
    )
    g2 = shifted(grad_in1, -1)
    out1 = call(
        forward_second,
        [VMEM] * 3 + [HBM, ANY],
        MESSAGE,
        [ROWS, PADDED, DENSE, MIXED, PAIR, WIDE, sems(1)],
        (act1, w, t, image_pair, grad_in1),
    )
    act2 = shifted(out1, 1)
    mine, theirs = call(
        taps_kernel,
        [VMEM] * 4 + [ANY],
        (
            jax.ShapeDtypeStruct((TAP_ROWS, HALF), f32),
            jax.ShapeDtypeStruct((TAP_ROWS, HALF), bf16),
        ),
        [PADDED, PADDED, pltpu.VMEM((TAP_ROWS, C), f32), WIDE],
        (pair, g0, g1, w, out1),
    )
    own_k, message = call(
        pack_kernel,
        [VMEM] * 3,
        (
            jax.ShapeDtypeStruct((TAP_ROWS, QUARTER), f32),
            jax.ShapeDtypeStruct((SECOND + LAST_ROWS, C), bf16),
        ),
        [],
        (mine, other_core(theirs), other_low),
    )
    low = other_chip(message)
    grad_out = call(
        functools.partial(unpack_kernel, is_last),
        [ANY, HBM, ANY],
        IMAGE,
        [pltpu.VMEM((PIX_ROWS, C), bf16), ROWS, PAIR, WIDE, sems(1)],
        (g2, head_pair, own_low),
    )
    act_out = call(
        functools.partial(unpack_kernel, is_first),
        [ANY, HBM, ANY],
        IMAGE,
        [MIXED, ROWS, PAIR, WIDE, sems(1)],
        (act2, image_pair, own_low),
    )
    grads = jax.ShapeDtypeStruct((QUARTER, C), f32)
    w_grad = call(
        final_first,
        [VMEM, VMEM],
        grads,
        [pltpu.VMEM((FIRST, C), f32), sems(1)],
        (own_top, top),
        outs=HBM,
    )
    w_grad, k_grad = call(
        final_second,
        [VMEM, VMEM, VMEM, ANY],
        (grads, jax.ShapeDtypeStruct((TAPS, 2, LANES), f32)),
        [pltpu.VMEM((SECOND, C), f32), pltpu.VMEM((TAP_ROWS, QUARTER), f32), sems(1)],
        (own_low, low, own_k, w_grad),
        outs=(HBM, VMEM),
        input_output_aliases={3: 0},
    )
    k_grad = k_grad.reshape(TAPS, QUARTER)
    return (act_out[None, None, None], grad_out[None, None, None], w_grad[None], k_grad[None])


def solution(mesh):
    in_specs = (
        P("section", "dp", None, None, None, None),
        P("section", "dp", None, None, None, None),
        P(None, "section", "dp", None, None, None, None),
        P(None, "dp", None, None, None, None),
        P(None, "dp", None, None, None, None),
        P("section", None, None),
        P("section", None, None),
    )
    out_specs = (
        P("section", "dp", None, None, None, None),
        P("section", "dp", None, None, None, None),
        P("section", "dp", None),
        P("section", None, "dp"),
    )
    return jax.shard_map(
        per_device, mesh=mesh, in_specs=in_specs, out_specs=out_specs, check_vma=False
    )
```

```python
import functools

import jax
import jax.numpy as jnp
from jax import lax
from jax.experimental import pallas as pl
from jax.experimental.pallas import tpu as pltpu
from jax.sharding import PartitionSpec as P

KW = 5
TAPS = KW * KW
TICKS = 2
HW = 14
PIX = HW * HW
PIX_ROWS = -(-PIX // 8) * 8
ACT_ROWS = 216
C = 1024
LANES = 128
GROUPS = C // LANES
ROW = HW * GROUPS
HALF = C // 2
QUARTER = C // 4
FIRST = 208
SECOND = QUARTER - FIRST
TAP_ROWS = 32
LAST_ROWS = TAP_ROWS // 4
PAD_ROWS = (HW + KW - 1) * ROW
DENSE_ROWS = PIX * GROUPS
TOP = (KW // 2) * ROW

f32 = jnp.float32
bf16 = jnp.bfloat16


def cols(group):
    return slice(group * LANES, (group + 1) * LANES)


def zero_pad(spread):
    zeros = jnp.zeros((TOP, LANES), f32)
    spread[0:TOP, :] = zeros
    spread[PAD_ROWS - TOP : PAD_ROWS, :] = zeros


def tile_at(spread, pixel):
    return spread[pl.ds(pl.multiple_of(pixel * GROUPS, GROUPS), GROUPS), :]


def conv(padded, taps, emit, flip):
    def row(p, carry):
        acc = [None] * HW
        for a in range(KW):
            tiles = [tile_at(padded, (p + a) * HW + q) for q in range(HW)]
            for b in range(KW):
                index = KW * a + b
                tap = taps[TAPS - 1 - index if flip else index]
                for q in range(HW):
                    src = q + b - KW // 2
                    if 0 <= src < HW:
                        term = tiles[src] * tap
                        acc[q] = term if acc[q] is None else acc[q] + term
        for q in range(HW):
            emit(p * HW + q, acc[q])
        return carry

    lax.fori_loop(0, HW, row, 0)


def tap_sums(rect_padded, grad_padded):
    def row(p, acc):
        acc = list(acc)
        grads = [tile_at(grad_padded, (p + KW // 2) * HW + q) for q in range(HW)]
        for a in range(KW):
            tiles = [tile_at(rect_padded, (p + a) * HW + q) for q in range(HW)]
            for b in range(KW):
                index = KW * a + b
                for q in range(HW):
                    src = q + b - KW // 2
                    if 0 <= src < HW:
                        acc[index] = acc[index] + tiles[src] * grads[q]
        return tuple(acc)

    return lax.fori_loop(0, HW, row, (jnp.zeros((GROUPS, LANES), f32),) * TAPS)


def store_tile(dense):
    def emit(pixel, value):
        dense[pl.ds(pl.multiple_of(pixel * GROUPS, GROUPS), GROUPS), :] = value

    return emit


def spread_rows(padded, group, value):
    padded[pl.ds(TOP + group, PIX, stride=GROUPS), :] = value


def rows_of(dense, group):
    return dense[pl.ds(group, PIX, stride=GROUPS), :]


def pack_rows(image, dst):
    for p in range(HW):
        dst[p * HW : (p + 1) * HW, :] = image[p].astype(f32)


def widen_pair(pair, wide):
    def step(p, carry):
        wide[pl.ds(pl.multiple_of(p * HW * 16, 16), HW * 16), :] = (
            pair[pl.ds(p * HW, HW)].astype(f32).reshape(HW * 16, LANES)
        )
        return carry

    lax.fori_loop(0, HW, step, 0)


def pair_tick_spread(wide, tick):
    return wide[pl.ds(tick, DENSE_ROWS, stride=TICKS), :]


def pair_tick_rows(wide, tick, group):
    return wide[pl.ds(tick + TICKS * group, PIX, stride=TICKS * GROUPS), :]


def replace_at_edge(edge, pair_hbm, tick, pair, wide, rows, sem):
    @pl.when(edge)
    def _():
        fetch(pair_hbm, pair, sem)
        widen_pair(pair, wide)
        for group in range(GROUPS):
            rows[:, cols(group)] = pair_tick_rows(wide, tick, group).astype(rows.dtype)


def fetch(src, dst, sem):
    copy = pltpu.make_async_copy(src, dst, sem)
    copy.start()
    copy.wait()


def is_first():
    return lax.axis_index("section") == 0


def is_last():
    return lax.axis_index("section") == lax.axis_size("section") - 1


def mix(rows, padded, dense, mixed, taps):
    zero_pad(padded)
    for group in range(GROUPS):
        spread_rows(padded, group, jnp.maximum(rows[:, cols(group)], 0.0))
    conv(padded, taps, store_tile(dense), False)
    for group in range(GROUPS):
        mixed[:, cols(group)] = rows_of(dense, group).astype(bf16)


def forward_first(x, weight, taps, token, out, rows, padded, dense, mixed):
    pack_rows(x, rows)
    mix(rows, padded, dense, mixed, taps)
    out[PIX:ACT_ROWS, :] = jnp.zeros((ACT_ROWS - PIX, C), bf16)
    out[0:PIX, :] = (rows[...] + jnp.dot(mixed[...], weight[...], preferred_element_type=f32)).astype(bf16)


def forward_second(x, weight, taps, images, token, out, rows, padded, dense, mixed, pair, wide, sem):
    rows[...] = x[0:PIX, :].astype(f32)
    replace_at_edge(is_first(), images, 0, pair, wide, rows, sem)
    mix(rows, padded, dense, mixed, taps)
    out[...] = (rows[...] + jnp.dot(mixed[...], weight[...], preferred_element_type=f32)).astype(bf16)


def head_kernel(g_in, heads, token, g_out, pair, wide, rows, sem):
    @pl.when(is_last())
    def _():
        fetch(heads, pair, sem)
        widen_pair(pair, wide)
        for group in range(GROUPS):
            rows[:, cols(group)] = pair_tick_rows(wide, 0, group).astype(bf16)
        fetch(rows, g_out, sem)


def spread_grad(g, weight, grad_mixed, waits=()):
    zero_pad(grad_mixed)
    for block in range(4):
        if waits:
            waits[block].wait()
        product = lax.dot_general(
            g[...],
            weight[block * QUARTER : (block + 1) * QUARTER, :],
            (((1,), (1,)), ((), ())),
            preferred_element_type=f32,
        )
        for part in range(2):
            spread_rows(grad_mixed, 2 * block + part, product[:, cols(part)])


def finish_backward(taps, out, grad_mixed, rows, dense, mask):
    def emit(pixel, value):
        keep = tile_at(mask, pixel) > 0.0
        store_tile(dense)(pixel, jnp.where(keep, value, 0.0))

    conv(grad_mixed, taps, emit, True)
    for group in range(GROUPS):
        out[0:PIX, cols(group)] = (rows[:, cols(group)] + rows_of(dense, group)).astype(bf16)


def backward_first(
    g_hbm, saved, w_hbm, taps_hbm, x_hbm, out, g_rows, weight, taps, pair, x, g, rows, grad_mixed, dense, mask, wide, sems
):
    blocks = [slice(block * QUARTER, (block + 1) * QUARTER) for block in range(4)]
    pieces = [(g_hbm, g)]
    pieces += [(w_hbm.at[rows_, :], weight.at[rows_, :]) for rows_ in blocks]
    pieces += [(saved, pair), (taps_hbm, taps), (x_hbm, x)]
    copies = [
        pltpu.make_async_copy(src, dst, sems.at[i]) for i, (src, dst) in enumerate(pieces)
    ]
    for copy in copies:
        copy.start()
    copies[0].wait()
    pack_rows(g, rows)
    g_rows[...] = rows[...].astype(bf16)
    spread_grad(g_rows, weight, grad_mixed, copies[1:5])
    copies[5].wait()
    widen_pair(pair, wide)
    mask[...] = pair_tick_spread(wide, 0)
    copies[6].wait()
    finish_backward(taps, out, grad_mixed, rows, dense, mask)
    copies[7].wait()


def backward_second(g, pair, weight, taps, token, out, rows, grad_mixed, dense, mask, wide):
    widen_pair(pair, wide)
    mask[...] = pair_tick_spread(wide, 1)
    rows[...] = g[...].astype(f32)
    spread_grad(g, weight, grad_mixed)
    out[PIX:PIX_ROWS, :] = jnp.zeros((PIX_ROWS - PIX, C), bf16)
    finish_backward(taps, out, grad_mixed, rows, dense, mask)


def factors_kernel(pair, g_rows, taps, token, keep, send, padded, dense, wide):
    core = lax.rem(lax.axis_index("dp"), 2)
    high = lax.div(lax.axis_index("dp"), 2)
    widen_pair(pair, wide)
    send[:, C : 2 * C] = g_rows[...]
    zero_pad(padded)
    for tick in range(TICKS):
        padded[TOP : TOP + DENSE_ROWS, :] = jnp.maximum(pair_tick_spread(wide, tick), 0.0)
        conv(padded, taps, store_tile(dense), False)
        for place in range(2):
            side = high if place == 0 else 1 - high
            for part in range(2):
                at = tick * HALF + (2 * place + part) * LANES
                mine = 4 * side + 2 * core + part
                theirs = 4 * side + 2 * (1 - core) + part
                keep[:, at : at + LANES] = rows_of(dense, mine).astype(bf16)
                send[:, at : at + LANES] = rows_of(dense, theirs).astype(bf16)


def weight_term(factor, grads):
    return lax.dot_general(factor, grads, (((0,), (0,)), ((), ())), preferred_element_type=f32)


def weight_first(keep, g_own, peer, out):
    out[...] = weight_term(keep[:, :HALF], g_own[...])
    out[...] += weight_term(peer[:, :HALF], peer[:, C : 2 * C])


def weight_second(total, keep, g_own, peer, g_peer, token, own_top, own_low, other_top, other_low):
    for place in range(2):
        rows = slice(place * QUARTER, (place + 1) * QUARTER)
        part = slice(HALF + place * QUARTER, HALF + (place + 1) * QUARTER)
        value = total[rows, :] + weight_term(keep[:, part], g_own[...])
        value += weight_term(peer[:, part], g_peer[...])
        if place == 0:
            own_top[...] = value[0:FIRST, :]
            own_low[...] = value[FIRST:QUARTER, :]
        else:
            other_top[...] = value[0:FIRST, :].astype(bf16)
            other_low[...] = value[FIRST:QUARTER, :].astype(bf16)


def taps_kernel(pair, g0, g1, weight, token, mine, theirs, rect, grad, sums, wide):
    core = lax.rem(lax.axis_index("dp"), 2)
    high = lax.div(lax.axis_index("dp"), 2)
    widen_pair(pair, wide)
    zero_pad(rect)
    for tick in range(TICKS):
        rect[TOP : TOP + DENSE_ROWS, :] = jnp.maximum(pair_tick_spread(wide, tick), 0.0)
        spread_grad((g0, g1)[tick], weight, grad)
        terms = tap_sums(rect, grad)
        if tick == 0:
            sums[TAPS:TAP_ROWS, :] = jnp.zeros((TAP_ROWS - TAPS, C), f32)
        for index in range(TAPS):
            row = jnp.concatenate([terms[index][i : i + 1] for i in range(GROUPS)], axis=1)
            if tick == 0:
                sums[index : index + 1, :] = row
            else:
                sums[index : index + 1, :] += row

    def block(side, which):
        at = pl.multiple_of((2 * side + which) * QUARTER, QUARTER)
        return sums[:, pl.ds(at, QUARTER)]

    for place in range(2):
        side = high if place == 0 else 1 - high
        at = slice(place * QUARTER, (place + 1) * QUARTER)
        mine[:, at] = block(side, core)
        theirs[:, at] = block(side, 1 - core).astype(bf16)


def pack_kernel(mine, arrived, other_low, own, message):
    total = mine[...] + arrived[...].astype(f32)
    own[...] = total[:, 0:QUARTER]
    message[0:SECOND, :] = other_low[...]
    for part in range(4):
        taps = total[part * LAST_ROWS : (part + 1) * LAST_ROWS, QUARTER:HALF]
        message[SECOND:, part * QUARTER : (part + 1) * QUARTER] = taps.astype(bf16)


SCALE = 1.0 / (2 * 2 * TICKS)


def final_first(own, top, out, rows, sem):
    rows[...] = (own[...] + top[...].astype(f32)) * SCALE
    fetch(rows, out.at[0:FIRST, :], sem)


def final_second(own, low, own_k, grads, out, out_k, rows, taps, sem):
    rows[...] = (own[...] + low[0:SECOND, :].astype(f32)) * SCALE
    copy = pltpu.make_async_copy(rows, out.at[FIRST:QUARTER, :], sem)
    copy.start()
    for part in range(4):
        at = slice(part * LAST_ROWS, (part + 1) * LAST_ROWS)
        arrived = low[SECOND:, part * QUARTER : (part + 1) * QUARTER].astype(f32)
        taps[at, :] = (own_k[at, :] + arrived) * SCALE
    for part in range(2):
        out_k[:, part, :] = taps[0:TAPS, cols(part)]
    copy.wait()


def unpack_kernel(edge, message, images, token, out, packed, rows, pair, wide, sem):
    fetch(message, packed, sem)
    rows[...] = packed[0:PIX, :].astype(f32)
    replace_at_edge(edge(), images, 1, pair, wide, rows, sem)
    for p in range(HW):
        out[p] = rows[p * HW : (p + 1) * HW, :].astype(bf16)


VMEM = pl.BlockSpec(memory_space=pltpu.VMEM)
HBM = pl.BlockSpec(memory_space=pltpu.HBM)
ANY = pl.BlockSpec(memory_space=pl.ANY)


def call(kernel, ins, out_shape, scratch, args, cost=1, outs=None, **options):
    pinned = [in_hbm(arg) if spec is HBM else arg for spec, arg in zip(ins, args)]
    return pl.pallas_call(
        kernel,
        in_specs=ins,
        out_specs=jax.tree.map(lambda _: VMEM, out_shape) if outs is None else outs,
        out_shape=out_shape,
        scratch_shapes=scratch,
        compiler_params=pltpu.CompilerParams(vmem_limit_bytes=20 * 1024 * 1024),
        cost_estimate=pl.CostEstimate(flops=0, bytes_accessed=cost << 10, transcendentals=0),
        **options,
    )(*pinned)


def in_hbm(array):
    return pltpu.with_memory_space_constraint(array, pltpu.HBM)


PAIR = pltpu.VMEM((PIX, TICKS * GROUPS, LANES), bf16)
WIDE = pltpu.VMEM((PIX * TICKS * GROUPS, LANES), f32)
ROWS = pltpu.VMEM((PIX, C), f32)
PADDED = pltpu.VMEM((PAD_ROWS, LANES), f32)
DENSE = pltpu.VMEM((DENSE_ROWS, LANES), f32)
MIXED = pltpu.VMEM((PIX, C), bf16)
TILED = pltpu.VMEM((HW, HW, C), bf16)
IMAGE = jax.ShapeDtypeStruct((HW, HW, C), bf16)
MESSAGE = jax.ShapeDtypeStruct((PIX, C), bf16)
LONGER = jax.ShapeDtypeStruct((PIX_ROWS, C), bf16)
ACTS = jax.ShapeDtypeStruct((ACT_ROWS, C), bf16)


def sems(count):
    return pltpu.SemaphoreType.DMA((count,)) if count > 1 else pltpu.SemaphoreType.DMA


def pair_view(array):
    moved = jnp.transpose(array, (1, 2, 0, 3)).reshape(HW, HW, TICKS, GROUPS, LANES)
    return jnp.transpose(moved, (0, 1, 3, 2, 4)).reshape(PIX, TICKS * GROUPS, LANES)


def shifted(value, by):
    peers = lax.axis_size("section")
    pairs = [(i, i + by) for i in range(peers) if 0 <= i + by < peers]
    return lax.ppermute(value, "section", pairs)


def other_core(value):
    return lax.ppermute(value, "dp", [(0, 1), (1, 0), (2, 3), (3, 2)])


def other_chip(value):
    return lax.ppermute(value, "dp", [(0, 2), (2, 0), (1, 3), (3, 1)])


def per_device(activations, incoming, saved, images, head_grads, pw_weight, dw_kernel):
    weight = pw_weight[0]
    taps = dw_kernel[0].reshape(TAPS, GROUPS, LANES)
    saved_pair = pair_view(saved[:, 0, 0, 0])
    image_pair = pair_view(images[:, 0, 0])
    head_pair = pair_view(head_grads[:, 0, 0])

    grad_in0, g0, w, t, pair, x0 = call(
        backward_first,
        [HBM] * 5,
        (MESSAGE, MESSAGE)
        + tuple(
            jax.ShapeDtypeStruct(shape, kind)
            for shape, kind in (
                ((C, C), bf16),
                ((TAPS, GROUPS, LANES), f32),
                (PAIR.shape, bf16),
                (TILED.shape, bf16),
            )
        ),
        [TILED, ROWS, PADDED, DENSE, DENSE, WIDE, sems(8)],
        (incoming[0, 0, 0], saved_pair, weight, taps, activations[0, 0, 0]),
    )
    g1 = shifted(grad_in0, -1)
    keep, send = call(
        factors_kernel,
        [VMEM, VMEM, VMEM, ANY],
        (MESSAGE, jax.ShapeDtypeStruct((PIX, 2 * C), bf16)),
        [PADDED, pltpu.VMEM((DENSE_ROWS + GROUPS, LANES), f32), WIDE],
        (pair, g0, t, grad_in0),
    )
    peer = other_core(send)
    out0 = call(
        forward_first,
        [VMEM, VMEM, VMEM, ANY],
        ACTS,
        [ROWS, PADDED, DENSE, MIXED],
        (x0, w, t, keep),
    )
    act1 = shifted(out0, 1)
    g1 = call(
        head_kernel,
        [ANY, HBM, ANY],
        MESSAGE,
        [PAIR, WIDE, MIXED, sems(1)],
        (g1, head_pair, out0),
        outs=ANY,
        input_output_aliases={0: 0},
    )
    g1_peer = other_core(g1)

    total = call(
        weight_first,
        [VMEM] * 3,
        jax.ShapeDtypeStruct((HALF, C), f32),
        [],
        (keep, g0, peer),
    )
    own_top, own_low, other_top, other_low = call(
        weight_second,
        [VMEM] * 5 + [ANY],
        (
            jax.ShapeDtypeStruct((FIRST, C), f32),
            jax.ShapeDtypeStruct((SECOND, C), f32),
            jax.ShapeDtypeStruct((FIRST, C), bf16),
            jax.ShapeDtypeStruct((SECOND, C), bf16),
        ),
        [],
        (total, keep, g1, peer, g1_peer, out0),
    )
    top = other_chip(other_top)
    grad_in1 = call(
        backward_second,
        [VMEM, VMEM, VMEM, VMEM, ANY],
        LONGER,
        [ROWS, PADDED, DENSE, DENSE, WIDE],
        (g1, pair, w, t, other_top),
    )
    g2 = shifted(grad_in1, -1)
    out1 = call(
        forward_second,
        [VMEM] * 3 + [HBM, ANY],
        MESSAGE,
        [ROWS, PADDED, DENSE, MIXED, PAIR, WIDE, sems(1)],
        (act1, w, t, image_pair, grad_in1),
    )
    act2 = shifted(out1, 1)
    mine, theirs = call(
        taps_kernel,
        [VMEM] * 4 + [ANY],
        (
            jax.ShapeDtypeStruct((TAP_ROWS, HALF), f32),
            jax.ShapeDtypeStruct((TAP_ROWS, HALF), bf16),
        ),
        [PADDED, PADDED, pltpu.VMEM((TAP_ROWS, C), f32), WIDE],
        (pair, g0, g1, w, out1),
    )
    own_k, message = call(
        pack_kernel,
        [VMEM] * 3,
        (
            jax.ShapeDtypeStruct((TAP_ROWS, QUARTER), f32),
            jax.ShapeDtypeStruct((SECOND + LAST_ROWS, C), bf16),
        ),
        [],
        (mine, other_core(theirs), other_low),
    )
    low = other_chip(message)
    grad_out = call(
        functools.partial(unpack_kernel, is_last),
        [ANY, HBM, ANY],
        IMAGE,
        [pltpu.VMEM((PIX_ROWS, C), bf16), ROWS, PAIR, WIDE, sems(1)],
        (g2, head_pair, own_low),
    )
    act_out = call(
        functools.partial(unpack_kernel, is_first),
        [ANY, HBM, ANY],
        IMAGE,
        [MIXED, ROWS, PAIR, WIDE, sems(1)],
        (act2, image_pair, own_low),
    )
    grads = jax.ShapeDtypeStruct((QUARTER, C), f32)
    w_grad = call(
        final_first,
        [VMEM, VMEM],
        grads,
        [pltpu.VMEM((FIRST, C), f32), sems(1)],
        (own_top, top),
        outs=HBM,
    )
    w_grad, k_grad = call(
        final_second,
        [VMEM, VMEM, VMEM, ANY],
        (grads, jax.ShapeDtypeStruct((TAPS, 2, LANES), f32)),
        [pltpu.VMEM((SECOND, C), f32), pltpu.VMEM((TAP_ROWS, QUARTER), f32), sems(1)],
        (own_low, low, own_k, w_grad),
        outs=(HBM, VMEM),
        input_output_aliases={3: 0},
    )
    k_grad = k_grad.reshape(TAPS, QUARTER)
    return (act_out[None, None, None], grad_out[None, None, None], w_grad[None], k_grad[None])


def solution(mesh):
    in_specs = (
        P("section", "dp", None, None, None, None),
        P("section", "dp", None, None, None, None),
        P(None, "section", "dp", None, None, None, None),
        P(None, "dp", None, None, None, None),
        P(None, "dp", None, None, None, None),
        P("section", None, None),
        P("section", None, None),
    )
    out_specs = (
        P("section", "dp", None, None, None, None),
        P("section", "dp", None, None, None, None),
        P("section", "dp", None),
        P("section", None, "dp"),
    )
    return jax.shard_map(
        per_device, mesh=mesh, in_specs=in_specs, out_specs=out_specs, check_vma=False
    )
```
